256 devices in a mesh: seq: 64 (over z, y, x_hi), dp: 4 (over x_lo, core).
Axes of the slice: x: 4 (x_hi: 2, x_lo: 2; x = x_hi * 2 + x_lo), y: 4, z: 8, core: 2. Of those that a mesh axis runs over, the one named last changes fastest.
Arguments:
- frames: float32 [4, 64, 192, 768], P('dp', 'seq'), may hold values from -6 to 6
- out_cotangent: float32 [4, 64, 192, 768], P('dp', 'seq'), may hold values from -0.6 to 0.6
- layer_norm_gain: float32 [768], replicated, may hold values from 0.5 to 1.5
- layer_norm_bias: float32 [768], replicated, may hold values from -1.2 to 1.2
- qkv_weight: float32 [768, 2304], P('seq'), may hold values from -2 to 2
- proj_weight: float32 [768, 768], P('seq'), may hold values from -0.21875 to 0.21875
- proj_bias: float32 [768], replicated, may hold values from -1.2 to 1.2
Outputs:
- frames_out: float32 [4, 64, 192, 768], P('dp', 'seq')
- grad_frames: float32 [4, 64, 192, 768], P('dp', 'seq')
- grad_ln_gain: float32 [768], replicated
- grad_ln_bias: float32 [768], replicated
- grad_qkv_weight: float32 [768, 2304], P('seq')
- grad_proj_weight: float32 [768, 768], P('seq')
- grad_proj_bias: float32 [768], replicated
The draws below stay inside these ranges and needn't reach their ends.
All inputs are finite; a program needn't handle non-finite values.
Results may differ from the reference program's by a relative error of at most 0.00015.
Values sent between devices are 32-bit elements; how exact they have to be, the bound alone decides.
A program may use at most 128 MiB of HBM per device.

```python
import math
import jax
import jax.numpy as jnp
from jax import lax

D = 768
HEADS = 12
HEAD_DIM = 64
PATCHES = 192
FRAMES = 64
CLIPS = 4


def draw_qkv_weight(key, part):
    key = jax.random.fold_in(key, 7)
    first = jax.random.fold_in(key, 0)
    whole = jax.random.normal(first, (D, 3 * D), jnp.float32) / math.sqrt(D)
    return jnp.clip(whole, -2.0, 2.0)


def level_of(own_key, shape, cuts, least, largest):
    def one(axis_at, blocks):
        heights = jax.random.uniform(jax.random.fold_in(jax.random.fold_in(own_key, 6), axis_at), (blocks,), jnp.float32, least / len(cuts), largest / len(cuts))
        return jnp.repeat(jnp.exp(heights), shape[axis_at] // blocks).reshape((-1,) + (1,) * (len(shape) - axis_at - 1))

    level = one(*cuts[0])
    for cut in cuts[1:]:
        level = level * one(*cut)
    return level


def bell_draw(key, extent, spread, most, pieces=(), dtype=jnp.bfloat16):
    values = jax.random.normal(key, extent, jnp.float32) * spread
    if len(pieces) > 0:
        values = level_of(key, extent, pieces, -0.22, 0.18) * values
    return jnp.clip(values, min=-most, max=most).astype(dtype)


def setup_inputs(seed: int = 0) -> dict:
    key_of = jax.random.split(jax.random.key(seed), 8)
    frames = bell_draw(key_of[0], (CLIPS, FRAMES, PATCHES, D), 1.0, 6.0, ((0, 4), (1, 64)), jnp.float32)
    out_cotangent = bell_draw(key_of[1], (CLIPS, FRAMES, PATCHES, D), 0.1, 0.6, ((0, 4), (1, 64)), jnp.float32)
    layer_norm_gain = jnp.clip(1.0 + 0.1 * jax.random.normal(key_of[2], (D,), jnp.float32), 0.5, 1.5)
    layer_norm_bias = bell_draw(key_of[3], (D,), 0.2, 1.2, (), jnp.float32)
    qkv_weight = draw_qkv_weight(jax.random.fold_in(key_of[7], 71), 0)
    proj_weight = bell_draw(key_of[5], (D, D), D ** -0.5, 0.21875, ((0, 64),), jnp.float32)
    proj_bias = bell_draw(key_of[6], (D,), 0.2, 1.2, (), jnp.float32)
    return dict(frames=frames, out_cotangent=out_cotangent, layer_norm_gain=layer_norm_gain, layer_norm_bias=layer_norm_bias, qkv_weight=qkv_weight, proj_weight=proj_weight, proj_bias=proj_bias)


EPSILON = 1e-06

def sub_block(clip, layer_norm_gain, layer_norm_bias, qkv_weight, proj_weight, proj_bias):
    highest = lax.Precision.HIGHEST
    frame_count = clip.shape[0]
    patch_count = clip.shape[1]
    row_average = lax.optimization_barrier(jnp.mean(clip, axis=-1, keepdims=True))
    centered_rows = clip - row_average
    inverse_deviation = lax.rsqrt(lax.optimization_barrier(jnp.mean(centered_rows * centered_rows, axis=-1, keepdims=True)) + EPSILON)
    norm_output = centered_rows * inverse_deviation * layer_norm_gain + layer_norm_bias
    qkv = jnp.dot(norm_output.reshape(-1, D), qkv_weight, precision=highest)
    qkv = qkv.reshape(frame_count, patch_count, 3, HEADS, HEAD_DIM)
    queries = qkv[:, :, 0]
    keys = qkv[:, :, 1]
    values = qkv[:, :, 2]
    scale = 1.0 / math.sqrt(HEAD_DIM)
    scores = jnp.einsum('tphd,fphd->phtf', queries, keys, precision=highest) * scale
    probs = jax.nn.softmax(scores, axis=-1)
    attended = jnp.einsum('phtf,fphd->tphd', probs, values, precision=highest).reshape(-1, D)
    projected = jnp.dot(attended, proj_weight, precision=highest) + proj_bias
    return clip + projected.reshape(clip.shape)

def reference(frames, out_cotangent, layer_norm_gain, layer_norm_bias, qkv_weight, proj_weight, proj_bias):

    def one_clip(pair):
        clip, cotangent = pair
        output, pull = jax.vjp(sub_block, clip, layer_norm_gain, layer_norm_bias, qkv_weight, proj_weight, proj_bias)
        grads = pull(cotangent)
        return (output,) + tuple(grads)
    result = lax.map(one_clip, (frames, out_cotangent))
    return (result[0], result[1], lax.optimization_barrier(jnp.sum(result[2], axis=0)), lax.optimization_barrier(jnp.sum(result[3], axis=0)), lax.optimization_barrier(jnp.sum(result[4], axis=0)), lax.optimization_barrier(jnp.sum(result[5], axis=0)), lax.optimization_barrier(jnp.sum(result[6], axis=0)))
```

```python
import functools
import math

import jax
import jax.numpy as jnp
from jax import lax
from jax.experimental import pallas as pl
from jax.experimental.pallas import tpu as pltpu
from jax.sharding import PartitionSpec as P

EPSILON = 1e-06
MESH = pl.DeviceIdType.MESH
F32 = jnp.float32
BF16 = jnp.bfloat16
WIDTH = 768
HALF = 384
LANES = 128


def position():
    s = lax.axis_index("seq")
    d = lax.axis_index("dp")
    return s, d, lax.div(s, 8), lax.rem(lax.div(s, 2), 4), lax.rem(s, 2), lax.div(d, 2), lax.rem(d, 2)


def device(s, d):
    return {"seq": s, "dp": d}


def greet(s, d, z, y, xh, xl, c):
    barrier = pltpu.get_barrier_semaphore()

    def one(k, carry):
        pl.semaphore_signal(barrier, inc=1, device_id=device(lax.rem(s + k, 64), d), device_id_type=MESH)
        return carry

    lax.fori_loop(1, 64, one, 0)
    mirror, side, mate = others(s, d, xh, xl, c)
    for where in (mirror, side, mate):
        pl.semaphore_signal(barrier, inc=1, device_id=where, device_id_type=MESH)
    pl.semaphore_wait(barrier, 66)


def others(s, d, xh, xl, c):
    mirror = device(s + 1 - 2 * xh, (1 - xl) * 2 + c)
    side = device(s, (1 - xl) * 2 + c)
    mate = device(s, xl * 2 + 1 - c)
    return mirror, side, mate


def send(src, dst, send_sem, recv_sem, where):
    copy = pltpu.make_async_remote_copy(
        src_ref=src, dst_ref=dst, send_sem=send_sem, recv_sem=recv_sem, device_id=where, device_id_type=MESH
    )
    copy.start()


def wait_for(ref, sem):
    pltpu.make_async_copy(ref, ref, sem).wait()


def bring_kernel(x_ref, dy_ref, wq_ref, wp_ref, xo, dyo, wqo, wpo, loc, ss, rx, rz, ry, rm, rs, rc):
    s, d, z, y, xh, xl, c = position()
    mirror, side, mate = others(s, d, xh, xl, c)
    greet(s, d, z, y, xh, xl, c)
    holds = lax.div(z, 4) == c
    zlow = lax.rem(z, 4)

    own_q = pltpu.make_async_copy(wq_ref, wqo.at[z, y, xh], rz.at[0])
    own_q.start()

    @pl.when(holds)
    def _():
        pltpu.make_async_copy(wp_ref, wpo.at[zlow, y, xh], rz.at[1]).start()

    def z_send(k, carry):
        there = device((lax.rem(z + k, 8) * 4 + y) * 2 + xh, d)
        send(wq_ref, wqo.at[z, y, xh], ss.at[0], rz.at[0], there)

        @pl.when(holds)
        def _():
            send(wp_ref, wpo.at[zlow, y, xh], ss.at[1], rz.at[1], there)

        return carry

    lax.fori_loop(1, 8, z_send, 0)

    pltpu.make_async_copy(x_ref.at[s], xo.at[c, s], rx.at[0]).start()
    pltpu.make_async_copy(dy_ref.at[s], dyo.at[c, s], rx.at[1]).start()

    def x_send(k, carry):
        t = lax.rem(s + k, 64)
        send(x_ref.at[t], xo.at[c, s], ss.at[2], rx.at[0], device(t, d))
        return carry

    lax.fori_loop(1, 64, x_send, 0)

    def dy_send(k, carry):
        t = lax.rem(s + k, 64)
        send(dy_ref.at[t], dyo.at[c, s], ss.at[3], rx.at[1], device(t, d))
        return carry

    lax.fori_loop(1, 64, dy_send, 0)

    wait_for(wqo.at[:, y, xh], rz.at[0])
    wait_for(wpo.at[:, y, xh], rz.at[1])

    for k in range(1, 4):
        there = device((z * 4 + lax.rem(y + k, 4)) * 2 + xh, d)
        send(wqo.at[:, y, xh], wqo.at[:, y, xh], ss.at[4], ry.at[0, k], there)
        send(wpo.at[:, y, xh], wpo.at[:, y, xh], ss.at[5], ry.at[1, k], there)

    give_q = pl.ds(4 * (1 - xl), 4)
    give_p = pl.ds(2 * (1 - xl), 2)
    take_q = pl.ds(4 * xl, 4)
    take_p = pl.ds(2 * xl, 2)

    def source(k):
        return lax.rem(y + 4 - k, 4)

    for k in range(4):
        at = source(k)
        if k > 0:
            wait_for(wqo.at[:, at, xh], ry.at[0, k])
            wait_for(wpo.at[:, at, xh], ry.at[1, k])
        send(wqo.at[give_q, at, xh], wqo.at[give_q, at, xh], ss.at[6], rm.at[0, k], mirror)
        send(wpo.at[give_p, at, xh], wpo.at[give_p, at, xh], ss.at[7], rm.at[1, k], mirror)
    for k in range(4):
        at = source(k)
        wait_for(wqo.at[take_q, at, 1 - xh], rm.at[0, k])
        wait_for(wpo.at[take_p, at, 1 - xh], rm.at[1, k])
        send(wqo.at[take_q, at, 1 - xh], wqo.at[take_q, at, 1 - xh], ss.at[8], rs.at[0, k], side)
        send(wpo.at[take_p, at, 1 - xh], wpo.at[take_p, at, 1 - xh], ss.at[9], rs.at[1, k], side)

    wait_for(xo.at[c], rx.at[0])
    send(xo.at[c], xo.at[c], ss.at[10], rc.at[0], mate)
    wait_for(dyo.at[c], rx.at[1])
    send(dyo.at[c], dyo.at[c], ss.at[11], rc.at[1], mate)

    for k in range(4):
        at = source(k)
        wait_for(wqo.at[give_q, at, 1 - xh], rs.at[0, k])
        wait_for(wpo.at[give_p, at, 1 - xh], rs.at[1, k])
    wait_for(xo.at[1 - c], rc.at[0])
    wait_for(dyo.at[1 - c], rc.at[1])

    wait_for(wqo.at[pl.ds(0, 7), 0, 0], ss.at[0])

    @pl.when(holds)
    def _():
        def w(k, carry):
            wait_for(wp_ref, ss.at[1])
            return carry

        lax.fori_loop(0, 7, w, 0)

    wait_for(xo.at[0, pl.ds(0, 63)], ss.at[2])
    wait_for(xo.at[0, pl.ds(0, 63)], ss.at[3])
    wait_for(wqo.at[:, pl.ds(0, 3), 0], ss.at[4])
    wait_for(wpo.at[:, pl.ds(0, 3), 0], ss.at[5])
    for sem in (6, 8):
        wait_for(wqo.at[pl.ds(0, 4), :, 0], ss.at[sem])
    for sem in (7, 9):
        wait_for(wpo.at[pl.ds(0, 2), :, 0], ss.at[sem])
    wait_for(xo.at[0], ss.at[10])
    wait_for(xo.at[0], ss.at[11])


def bring(x, dy, wq, wp):
    dma = pltpu.SemaphoreType.DMA
    anywhere = pl.BlockSpec(memory_space=pl.ANY)
    return pl.pallas_call(
        bring_kernel,
        out_shape=(
            jax.ShapeDtypeStruct((2, 64, 9, 2, LANES), F32),
            jax.ShapeDtypeStruct((2, 64, 9, 2, LANES), F32),
            jax.ShapeDtypeStruct((8, 4, 2, 27, 4, LANES), F32),
            jax.ShapeDtypeStruct((4, 4, 2, 9, 8, LANES), F32),
        ),
        in_specs=[anywhere] * 4,
        out_specs=(anywhere,) * 4,
        scratch_shapes=[
            dma((2,)), dma((12,)), dma((2,)), dma((2,)), dma((2, 4)), dma((2, 4)), dma((2, 4)), dma((2,)),
        ],
        compiler_params=pltpu.CompilerParams(collective_id=0, has_side_effects=True),
    )(x, dy, wq, wp)


def split(v):
    high = v.astype(BF16)
    return high, (v - high.astype(F32)).astype(BF16)


def mm(a, b, ca, cb):
    return lax.dot_general(a, b, (((ca,), (cb,)), ((), ())), preferred_element_type=F32)


def mm3(a, b, ca, cb):
    return mm(a[0], b[0], ca, cb) + (mm(a[1], b[0], ca, cb) + mm(a[0], b[1], ca, cb))


def compute_kernel(
    x_ref, dy_ref, wq_ref, wp_ref, gain_ref, bias_ref,
    out_ref, dx_ref, gq_ref, gp_ref, small_ref,
    xhat, rstd, nh, nl, yh, yl, wh, wl, ph, plo, qkv, da, ah, al, dh, dl,
):
    cols = [slice(LANES * j, LANES * (j + 1)) for j in range(9)]
    gain = gain_ref[...]
    bias = bias_ref[...]
    for j in range(9):
        wh[:, cols[j]], wl[:, cols[j]] = split(wq_ref[pl.ds(j, WIDTH, stride=9), :])
    for j in range(6):
        ph[:, cols[j]], plo[:, cols[j]] = split(wp_ref[pl.ds(j, HALF, stride=6), :])
    dy_sum = jnp.zeros((1, WIDTH), F32)
    for g in range(6):
        base = (g // 3) * 1152 + (g % 3) * 6
        rows = slice(64 * g, 64 * (g + 1))
        x = jnp.concatenate([x_ref[pl.ds(base + j, 64, stride=18), :] for j in range(6)], axis=1)
        centred = x - jnp.mean(x, axis=1, keepdims=True)
        r = lax.rsqrt(jnp.mean(centred * centred, axis=1, keepdims=True) + EPSILON)
        hat = centred * r
        xhat[rows, :] = hat
        rstd[rows, :] = jnp.broadcast_to(r, (64, LANES))
        nh[rows, :], nl[rows, :] = split(hat * gain + bias)
        y = jnp.concatenate([dy_ref[pl.ds(base + j, 64, stride=18), :] for j in range(6)], axis=1)
        yh[rows, :], yl[rows, :] = split(y)
        dy_sum = dy_sum + jnp.sum(y, axis=0, keepdims=True)
    for t in range(3):
        part = slice(HALF * t, HALF * (t + 1))
        qkv[:, part] = mm3((nh[...], nl[...]), (wh[:, part], wl[:, part]), 1, 0)
    da[...] = mm3((yh[...], yl[...]), (ph[...], plo[...]), 1, 1)
    left = lax.broadcasted_iota(jnp.int32, (LANES, LANES), 1) < 64
    row = lax.broadcasted_iota(jnp.int32, (2 * LANES, LANES), 0)
    col = lax.broadcasted_iota(jnp.int32, (2 * LANES, LANES), 1)
    same = ((row % LANES) < 64) == (col < 64)

    def stacked(v):
        return jnp.concatenate([jnp.where(left, v, 0.0), jnp.where(left, 0.0, v)], axis=0)

    def joined(v):
        return jnp.where(left, v[:LANES], v[LANES:])

    scale = 0.125
    for i in range(3):
        rows = slice(LANES * i, LANES * (i + 1))
        for h in range(3):
            q = split(stacked(qkv[rows, cols[h]] * scale))
            k = split(qkv[rows, cols[3 + h]])
            v = split(qkv[rows, cols[6 + h]])
            a = split(stacked(da[rows, cols[h]]))
            scores = jnp.where(same, mm3(q, k, 1, 1), -1e30)
            e = jnp.exp(scores - jnp.max(scores, axis=1, keepdims=True))
            probs = e / jnp.sum(e, axis=1, keepdims=True)
            pair = split(probs)
            ah[rows, cols[h]], al[rows, cols[h]] = split(joined(mm3(pair, v, 1, 0)))
            dh[rows, cols[6 + h]], dl[rows, cols[6 + h]] = split(mm3(pair, a, 0, 0))
            t = mm3(a, v, 1, 1) * probs
            ds = split(t - probs * jnp.sum(t, axis=1, keepdims=True))
            dh[rows, cols[h]], dl[rows, cols[h]] = split(joined(mm3(ds, k, 1, 0)) * scale)
            dh[rows, cols[3 + h]], dl[rows, cols[3 + h]] = split(mm3(ds, q, 0, 0))
    for t in range(2):
        part = slice(HALF * t, HALF * (t + 1))
        o = mm3((ah[...], al[...]), (ph[:, part], plo[:, part]), 1, 0)
        for g in range(6):
            for j in range(3):
                out_ref[pl.ds((g // 3) * 1152 + (g % 3) * 6 + 3 * t + j, 64, stride=18), :] = (
                    o[64 * g : 64 * (g + 1), cols[j]]
                )
        w = mm3((ah[...], al[...]), (yh[:, part], yl[:, part]), 0, 0)
        for j in range(3):
            gp_ref[pl.ds(3 * t + j, HALF, stride=6), :] = w[:, cols[j]]
    for t in range(3):
        part = slice(HALF * t, HALF * (t + 1))
        w = mm3((nh[...], nl[...]), (dh[:, part], dl[:, part]), 0, 0)
        for j in range(3):
            gq_ref[pl.ds(3 * t + j, WIDTH, stride=9), :] = w[:, cols[j]]
    gain_sum = jnp.zeros((1, WIDTH), F32)
    bias_sum = jnp.zeros((1, WIDTH), F32)
    for i in range(3):
        dn = mm3((dh[128 * i : 128 * (i + 1), :], dl[128 * i : 128 * (i + 1), :]), (wh[...], wl[...]), 1, 1)
        for half in range(2):
            g = 2 * i + half
            rows = slice(64 * g, 64 * (g + 1))
            n = dn[64 * half : 64 * (half + 1)]
            hat = xhat[rows, :]
            gain_sum = gain_sum + jnp.sum(n * hat, axis=0, keepdims=True)
            bias_sum = bias_sum + jnp.sum(n, axis=0, keepdims=True)
            n = n * gain
            m1 = jnp.mean(n, axis=1, keepdims=True)
            m2 = jnp.mean(n * hat, axis=1, keepdims=True)
            r = rstd[rows, 0:1]
            dx = r * (n - m1 - hat * m2)
            for j in range(6):
                dx_ref[pl.ds((g // 3) * 1152 + (g % 3) * 6 + j, 64, stride=18), :] = dx[:, cols[j]]
    for n, v in enumerate((gain_sum, bias_sum, dy_sum * 0.5)):
        for j in range(6):
            small_ref[6 * n + j : 6 * n + j + 1, :] = v[:, cols[j]]
    small_ref[18:24, :] = jnp.zeros((6, LANES), F32)


def compute(x, dy, wq, wp, gain, bias):
    vmem = pl.BlockSpec(memory_space=pltpu.VMEM)
    tokens = HALF
    return pl.pallas_call(
        compute_kernel,
        out_shape=(
            jax.ShapeDtypeStruct((2304, LANES), F32),
            jax.ShapeDtypeStruct((2304, LANES), F32),
            jax.ShapeDtypeStruct((6912, LANES), F32),
            jax.ShapeDtypeStruct((2304, LANES), F32),
            jax.ShapeDtypeStruct((24, LANES), F32),
        ),
        in_specs=[vmem] * 6,
        out_specs=(vmem,) * 5,
        scratch_shapes=[
            pltpu.VMEM((tokens, WIDTH), F32),
            pltpu.VMEM((tokens, LANES), F32),
            pltpu.VMEM((tokens, WIDTH), BF16),
            pltpu.VMEM((tokens, WIDTH), BF16),
            pltpu.VMEM((tokens, WIDTH), BF16),
            pltpu.VMEM((tokens, WIDTH), BF16),
            pltpu.VMEM((WIDTH, 3 * HALF), BF16),
            pltpu.VMEM((WIDTH, 3 * HALF), BF16),
            pltpu.VMEM((HALF, WIDTH), BF16),
            pltpu.VMEM((HALF, WIDTH), BF16),
            pltpu.VMEM((tokens, 3 * HALF), F32),
            pltpu.VMEM((tokens, HALF), F32),
            pltpu.VMEM((tokens, HALF), BF16),
            pltpu.VMEM((tokens, HALF), BF16),
            pltpu.VMEM((tokens, 3 * HALF), BF16),
            pltpu.VMEM((tokens, 3 * HALF), BF16),
        ],
        compiler_params=pltpu.CompilerParams(vmem_limit_bytes=50 * 1024 * 1024),
    )(x, dy, wq, wp, gain, bias)


def give_kernel(
    o_ref, dx_ref, gq_ref, gp_ref, sm_ref, of, df, rq, rp, so,
    ob, db, q1, p1, q2, p2, qa, pa, qy, py, qz, pz, qf, pf, qs, ps, pt, smx, smy, smz, sms, smc,
    ss, rb, r1, r2, ry, rz, rs, rc, ro, sa, ra,
):
    s, d, z, y, xh, xl, c = position()
    mirror, side, mate = others(s, d, xh, xl, c)
    greet(s, d, z, y, xh, xl, c)
    holds = lax.div(z, 4) == c
    mine_q, mine_p = 4 * xl, 2 * xl
    yours_q, yours_p = 4 * (1 - xl), 2 * (1 - xl)
    oxh = 1 - xh

    def ydst(k):
        return lax.rem(y + k, 4)

    order = (1, 2, 3, 0)
    for k in order:
        at = ydst(k)
        send(gq_ref.at[pl.ds(yours_q, 4), at, oxh], q1.at[k], ss.at[0], r1.at[0, k], side)
        send(gp_ref.at[pl.ds(yours_p, 2), at, oxh], p1.at[k], ss.at[1], r1.at[1, k], side)
    send(o_ref.at[1 - c], ob, ss.at[2], rb.at[0], mate)
    send(dx_ref.at[1 - c], db, ss.at[3], rb.at[1], mate)
    smx[0] = sm_ref[...]
    send(smx.at[0], smx.at[1], ss.at[4], ra.at[0], mirror)

    def back(own, buf, out, k_recv, k_send, k_out):
        wait_for(buf, rb.at[k_recv])

        def add(i, carry):
            buf[i] = buf[i] + own[c, i]
            return carry

        lax.fori_loop(0, 64, add, 0)
        pltpu.make_async_copy(buf.at[s], out.at[s], ro.at[k_out]).start()

        def one(k, carry):
            t = lax.rem(s + k, 64)
            send(buf.at[t], out.at[s], ss.at[k_send], ro.at[k_out], device(t, d))
            return carry

        lax.fori_loop(1, 64, one, 0)

    for k in order:
        at = ydst(k)
        wait_for(q1.at[k], r1.at[0, k])
        wait_for(p1.at[k], r1.at[1, k])

        for i in range(4):
            q1[k, i] = q1[k, i] + gq_ref[mine_q + i, at, oxh]
        for i in range(2):
            p1[k, i] = p1[k, i] + gp_ref[mine_p + i, at, oxh]
        send(q1.at[k], q2.at[k], ss.at[5], r2.at[0, k], mirror)
        send(p1.at[k], p2.at[k], ss.at[6], r2.at[1, k], mirror)
        if k == 1:
            back(o_ref, ob, of, 0, 7, 0)
        if k == 2:
            back(dx_ref, db, df, 1, 8, 1)

    wait_for(smx.at[1], ra.at[0])
    smy[y] = smx[0] + smx[1]
    for k in range(1, 4):
        there = device((z * 4 + ydst(k)) * 2 + xh, d)
        send(smy.at[y], smy.at[y], ss.at[9], ra.at[1], there)

    for k in order:
        at = ydst(k)
        wait_for(q2.at[k], r2.at[0, k])
        wait_for(p2.at[k], r2.at[1, k])
        for i in range(4):
            qa[k, yours_q + i] = q2[k, i] + gq_ref[yours_q + i, at, xh]
            qa[k, mine_q + i] = gq_ref[mine_q + i, at, xh]
        for i in range(2):
            pa[k, yours_p + i] = p2[k, i] + gp_ref[yours_p + i, at, xh]
            pa[k, mine_p + i] = gp_ref[mine_p + i, at, xh]
        if k > 0:
            there = device((z * 4 + at) * 2 + xh, d)
            send(qa.at[k], qy.at[k], ss.at[10], ry.at[0, k], there)
            send(pa.at[k], py.at[k], ss.at[11], ry.at[1, k], there)

    wait_for(smy.at[pl.ds(0, 3)], ra.at[1])
    smz[z] = (smy[0] + smy[1]) + (smy[2] + smy[3])

    def sz(k, carry):
        there = device((lax.rem(z + k, 8) * 4 + y) * 2 + xh, d)
        send(smz.at[z], smz.at[z], ss.at[12], ra.at[2], there)
        return carry

    lax.fori_loop(1, 8, sz, 0)

    for k in range(1, 4):
        wait_for(qy.at[k], ry.at[0, k])
        wait_for(py.at[k], ry.at[1, k])

    def zq(i, carry):
        qa[0, i] = (qa[0, i] + qy[1, i]) + (qy[2, i] + qy[3, i])
        return carry

    lax.fori_loop(0, 8, zq, 0)

    def zp(i, carry):
        pa[0, i] = (pa[0, i] + py[1, i]) + (py[2, i] + py[3, i])
        return carry

    lax.fori_loop(0, 4, zp, 0)

    def zs(k, carry):
        at = lax.rem(z + k, 8)
        there = device((at * 4 + y) * 2 + xh, d)
        send(qa.at[0, at], qz.at[z], ss.at[13], rz.at[0], there)

        @pl.when(lax.div(at, 4) == c)
        def _():
            send(pa.at[0, lax.rem(at, 4)], pz.at[z], ss.at[14], rz.at[1], there)

        return carry

    lax.fori_loop(1, 8, zs, 0)
    qz[z] = qa[0, z]

    @pl.when(holds)
    def _():
        pz[z] = pa[0, lax.rem(z, 4)]

    wait_for(smz.at[pl.ds(0, 7)], ra.at[2])
    total = ((smz[0] + smz[1]) + (smz[2] + smz[3])) + ((smz[4] + smz[5]) + (smz[6] + smz[7]))
    sms[0] = total
    send(sms.at[0], sms.at[1], ss.at[15], ra.at[3], side)

    wait_for(qz.at[pl.ds(0, 7)], rz.at[0])
    qf[...] = ((qz[0] + qz[1]) + (qz[2] + qz[3])) + ((qz[4] + qz[5]) + (qz[6] + qz[7]))
    send(qf, qs, ss.at[16], rs.at[0], side)

    @pl.when(holds)
    def _():
        wait_for(pz.at[pl.ds(0, 7)], rz.at[1])
        pf[...] = ((pz[0] + pz[1]) + (pz[2] + pz[3])) + ((pz[4] + pz[5]) + (pz[6] + pz[7]))
        send(pf, ps, ss.at[17], rs.at[1], side)

    wait_for(sms.at[1], ra.at[3])
    smc[0] = sms[0] + sms[1]
    send(smc.at[0], smc.at[1], ss.at[18], ra.at[4], mate)
    wait_for(qs, rs.at[0])
    wait_for(qf, ss.at[16])
    qf[...] = qf[...] + qs[...]
    keep = pltpu.make_async_copy(qf, rq.at[c], sa.at[0])
    keep.start()
    send(qf, rq.at[c], ss.at[19], rc.at[0], mate)

    @pl.when(holds)
    def _():
        wait_for(ps, rs.at[1])
        pt[...] = pf[...] + ps[...]
        pltpu.make_async_copy(pt, rp, sa.at[1]).start()
        send(pt, rp, ss.at[20], rc.at[1], mate)

    wait_for(smc.at[1], ra.at[4])
    so[...] = smc[0] + smc[1]
    wait_for(qf, rc.at[0])
    keep.wait()

    @pl.when(holds)
    def _():
        wait_for(pt, sa.at[1])
        wait_for(pt, ss.at[20])
        wait_for(pf, ss.at[17])
        wait_for(pz.at[pl.ds(0, 3)], ss.at[14])

    @pl.when(jnp.logical_not(holds))
    def _():
        wait_for(pt, rc.at[1])
        wait_for(pz.at[pl.ds(0, 4)], ss.at[14])

    wait_for(ob, ro.at[0])
    wait_for(db, ro.at[1])
    wait_for(q1, ss.at[0])
    wait_for(p1, ss.at[1])
    wait_for(ob, ss.at[2])
    wait_for(db, ss.at[3])
    wait_for(smx.at[0], ss.at[4])
    wait_for(q2, ss.at[5])
    wait_for(p2, ss.at[6])
    wait_for(ob.at[pl.ds(0, 63)], ss.at[7])
    wait_for(db.at[pl.ds(0, 63)], ss.at[8])
    wait_for(smy.at[pl.ds(0, 3)], ss.at[9])
    wait_for(qa.at[pl.ds(1, 3)], ss.at[10])
    wait_for(pa.at[pl.ds(1, 3)], ss.at[11])
    wait_for(smz.at[pl.ds(0, 7)], ss.at[12])
    wait_for(qz.at[pl.ds(0, 7)], ss.at[13])
    wait_for(sms.at[0], ss.at[15])
    wait_for(smc.at[0], ss.at[18])
    wait_for(qf, ss.at[19])


def give(o, dx, gq, gp, sm):
    dma = pltpu.SemaphoreType.DMA
    anywhere = pl.BlockSpec(memory_space=pl.ANY)
    vmem = pl.BlockSpec(memory_space=pltpu.VMEM)
    act = (64, 9, 2, LANES)
    q, p, sml = (27, 4, LANES), (9, 8, LANES), (24, LANES)

    def buf(*shape):
        return pltpu.VMEM(shape, F32)

    return pl.pallas_call(
        give_kernel,
        out_shape=(
            jax.ShapeDtypeStruct(act, F32),
            jax.ShapeDtypeStruct(act, F32),
            jax.ShapeDtypeStruct((2,) + q, F32),
            jax.ShapeDtypeStruct(p, F32),
            jax.ShapeDtypeStruct(sml, F32),
        ),
        in_specs=[vmem] * 5,
        out_specs=(anywhere, anywhere, anywhere, anywhere, vmem),
        scratch_shapes=[
            buf(*act), buf(*act),
            buf(4, 4, *q), buf(4, 2, *p), buf(4, 4, *q), buf(4, 2, *p),
            buf(4, 8, *q), buf(4, 4, *p), buf(4, 8, *q), buf(4, 4, *p),
            buf(8, *q), buf(8, *p), buf(*q), buf(*p), buf(*q), buf(*p), buf(*p),
            buf(2, *sml), buf(4, *sml), buf(8, *sml), buf(2, *sml), buf(2, *sml),
            dma((21,)), dma((2,)), dma((2, 4)), dma((2, 4)), dma((2, 4)), dma((2,)), dma((2,)), dma((2,)),
            dma((2,)), dma((2,)), dma((5,)),
        ],
        compiler_params=pltpu.CompilerParams(
            collective_id=1, has_side_effects=True, vmem_limit_bytes=50 * 1024 * 1024
        ),
    )(o, dx, gq, gp, sm)


def on_device(
    frames, out_cotangent, layer_norm_gain, layer_norm_bias, qkv_weight, proj_weight, proj_bias
):
    c = lax.rem(lax.axis_index("dp"), 2)
    blocks = (64, 9, 2, LANES)
    half = lax.dynamic_index_in_dim(qkv_weight.reshape(12, 3, 2, HALF), c, axis=2, keepdims=False)
    x, dy, wq, wp = bring(
        frames.reshape(blocks),
        out_cotangent.reshape(blocks),
        half.reshape(27, 4, LANES),
        proj_weight.reshape(9, 8, LANES),
    )
    o, dx, gq, gp, small = compute(
        x.reshape(2304, LANES),
        dy.reshape(2304, LANES),
        wq.reshape(6912, LANES),
        wp.reshape(2304, LANES),
        layer_norm_gain.reshape(1, WIDTH),
        layer_norm_bias.reshape(1, WIDTH),
    )
    of, df, rq, rp, so = give(
        o.reshape((2,) + blocks),
        dx.reshape((2,) + blocks),
        gq.reshape(8, 4, 2, 27, 4, LANES),
        gp.reshape(4, 4, 2, 9, 8, LANES),
        small,
    )
    sums = so[:18].reshape(3, WIDTH)
    grad_qkv = jnp.transpose(rq.reshape(2, 12, 3, HALF), (1, 2, 0, 3)).reshape(12, 3 * WIDTH)
    return (
        frames + of.reshape(frames.shape) + proj_bias,
        out_cotangent + df.reshape(frames.shape),
        sums[0],
        sums[1],
        grad_qkv,
        rp.reshape(12, WIDTH),
        sums[2],
    )


def solution(mesh):
    return jax.shard_map(
        on_device,
        mesh=mesh,
        in_specs=(
            P("dp", "seq", None, None),
            P("dp", "seq", None, None),
            P(),
            P(),
            P("seq", None),
            P("seq", None),
            P(),
        ),
        out_specs=(
            P("dp", "seq", None, None),
            P("dp", "seq", None, None),
            P(),
            P(),
            P("seq", None),
            P("seq", None),
            P(),
        ),
        check_vma=False,
    )
```

```python
import functools
import math

import jax
import jax.numpy as jnp
from jax import lax
from jax.experimental import pallas as pl
from jax.experimental.pallas import tpu as pltpu
from jax.sharding import PartitionSpec as P

EPSILON = 1e-06
MESH = pl.DeviceIdType.MESH
F32 = jnp.float32
BF16 = jnp.bfloat16
WIDTH = 768
HALF = 384
LANES = 128


def position():
    s = lax.axis_index("seq")
    d = lax.axis_index("dp")
    return s, d, lax.div(s, 8), lax.rem(lax.div(s, 2), 4), lax.rem(s, 2), lax.div(d, 2), lax.rem(d, 2)


def device(s, d):
    return {"seq": s, "dp": d}


def greet(s, d, z, y, xh, xl, c, *more):
    barrier = pltpu.get_barrier_semaphore()

    def one(k, carry):
        pl.semaphore_signal(barrier, inc=1, device_id=device(lax.rem(s + k, 64), d), device_id_type=MESH)
        return carry

    lax.fori_loop(1, 64, one, 0)
    near = others(s, d, xh, xl, c) + more
    for where in near:
        pl.semaphore_signal(barrier, inc=1, device_id=where, device_id_type=MESH)
    pl.semaphore_wait(barrier, 63 + len(near))


def others(s, d, xh, xl, c):
    mirror = device(s + 1 - 2 * xh, (1 - xl) * 2 + c)
    side = device(s, (1 - xl) * 2 + c)
    mate = device(s, xl * 2 + 1 - c)
    return mirror, side, mate


def send(src, dst, send_sem, recv_sem, where):
    copy = pltpu.make_async_remote_copy(
        src_ref=src, dst_ref=dst, send_sem=send_sem, recv_sem=recv_sem, device_id=where, device_id_type=MESH
    )
    copy.start()


def wait_for(ref, sem):
    pltpu.make_async_copy(ref, ref, sem).wait()


ORDER = (0, 1, 7, 2, 6, 3, 5, 4)


def bring_kernel(x_ref, dy_ref, wq_ref, wp_ref, xo, dyo, wqo, wpo, ss, rx, rz, ry, rm, rs, rc):
    s, d, z, y, xh, xl, c = position()
    mirror, side, mate = others(s, d, xh, xl, c)
    greet(s, d, z, y, xh, xl, c)

    def zdev(k):
        return device((lax.rem(z + k + 8, 8) * 4 + y) * 2 + xh, d)

    def ydev(k):
        return device((z * 4 + lax.rem(y + k, 4)) * 2 + xh, d)

    def both(j, q_job, p_job):
        at = lax.rem(z + j, 8)
        q_job(at)

        @pl.when(lax.div(at, 4) == c)
        def _():
            p_job(lax.rem(at, 4))

    def along_z(j, to, there, src_q=None, src_p=None):
        both(
            j,
            lambda at: send(wqo.at[at, y, xh] if src_q is None else src_q, wqo.at[at, y, xh], ss.at[0], rz.at[0, to], there),
            lambda at: send(wpo.at[at, y, xh] if src_p is None else src_p, wpo.at[at, y, xh], ss.at[1], rz.at[1, to], there),
        )

    def z_stage(j):
        if j == 0:
            along_z(0, 7, zdev(1), wq_ref, wp_ref)
            along_z(0, 1, zdev(-1), wq_ref, wp_ref)
            both(
                0,
                lambda at: pltpu.make_async_copy(wq_ref, wqo.at[at, y, xh], rz.at[0, 0]).start(),
                lambda at: pltpu.make_async_copy(wp_ref, wpo.at[at, y, xh], rz.at[1, 0]).start(),
            )
        both(
            j,
            lambda at: wait_for(wqo.at[at, y, xh], rz.at[0, j]),
            lambda at: wait_for(wpo.at[at, y, xh], rz.at[1, j]),
        )
        if j in (7, 6):
            along_z(j, j - 1, zdev(1))
        if j in (1, 2):
            along_z(j, j + 1, zdev(-1))
        if j == 5:
            @pl.when(c == 0)
            def _():
                along_z(5, 4, zdev(1))
        if j == 3:
            @pl.when(c == 1)
            def _():
                along_z(3, 4, zdev(-1))

    def y_send(j):
        for k in (1, 3):
            both(
                j,
                lambda at: send(wqo.at[at, y, xh], wqo.at[at, y, xh], ss.at[4], ry.at[0, j, k], ydev(k)),
                lambda at: send(wpo.at[at, y, xh], wpo.at[at, y, xh], ss.at[5], ry.at[1, j, k], ydev(k)),
            )

    def across(j, k):
        row = lax.rem(y + 4 - k, 4)
        hq, hp = pl.ds(27 * (1 - xl), 27), pl.ds(9 * (1 - xl), 9)

        def q(at):
            ref = wqo.at[at, row, xh, hq]
            send(ref, ref, ss.at[6], rm.at[0, j, row], mirror)

        def p(at):
            ref = wpo.at[at, row, xh, hp]
            send(ref, ref, ss.at[7], rm.at[1, j, row], mirror)

        both(j, q, p)

    def y_wait(j, k):
        row = lax.rem(y + 4 - k, 4)
        both(
            j,
            lambda at: wait_for(wqo.at[at, row, xh], ry.at[0, j, k]),
            lambda at: wait_for(wpo.at[at, row, xh], ry.at[1, j, k]),
        )

    def y_pass(j, k):
        h = 0 if k == 1 else 1
        row = lax.rem(y + 4 - k, 4)

        def q(at):
            ref = wqo.at[at, row, xh, pl.ds(27 * h, 27)]
            send(ref, ref, ss.at[4], ry.at[0, j, 2], ydev(k))

        def p(at):
            ref = wpo.at[at, row, xh, pl.ds(9 * h, 9)]
            send(ref, ref, ss.at[5], ry.at[1, j, 2], ydev(k))

        both(j, q, p)

    def forward(j, k):
        row = lax.rem(y + 4 - k, 4)
        hq, hp = pl.ds(27 * xl, 27), pl.ds(9 * xl, 9)

        def q(at):
            ref = wqo.at[at, row, 1 - xh, hq]
            wait_for(ref, rm.at[0, j, row])
            send(ref, ref, ss.at[8], rs.at[0, j, row], side)

        def p(at):
            ref = wpo.at[at, row, 1 - xh, hp]
            wait_for(ref, rm.at[1, j, row])
            send(ref, ref, ss.at[9], rs.at[1, j, row], side)

        both(j, q, p)

    pltpu.make_async_copy(x_ref.at[s], xo.at[c, s], rx.at[0]).start()
    pltpu.make_async_copy(dy_ref.at[s], dyo.at[c, s], rx.at[1]).start()

    def spread(n, first, last):
        src, dst = ((x_ref, xo), (dy_ref, dyo))[n]

        def one(k, carry):
            t = lax.rem(s + k, 64)
            send(src.at[t], dst.at[c, s], ss.at[2 + n], rx.at[n], device(t, d))
            return carry

        lax.fori_loop(first, last, one, 0)

    for t in range(11):
        if t < 8:
            z_stage(ORDER[t])
            y_send(ORDER[t])
            across(ORDER[t], 0)
        if 1 <= t < 9:
            j = ORDER[t - 1]
            for k in (1, 3):
                y_wait(j, k)
                y_pass(j, k)
                across(j, k)
        if 2 <= t < 10:
            j = ORDER[t - 2]
            y_wait(j, 2)
            across(j, 2)
            forward(j, 0)
        if 3 <= t < 11:
            j = ORDER[t - 3]
            for k in (1, 3, 2):
                forward(j, k)
        if t == 1:
            spread(0, 1, 17)
        if t == 2:
            spread(0, 17, 33)
        if t == 3:
            spread(0, 33, 49)
        if t == 4:
            spread(0, 49, 64)
        if t == 5:
            spread(1, 1, 17)
        if t == 6:
            spread(1, 17, 33)
        if t == 7:
            spread(1, 33, 49)
        if t == 8:
            spread(1, 49, 64)

    wait_for(xo.at[c], rx.at[0])
    send(xo.at[c], xo.at[c], ss.at[10], rc.at[0], mate)
    wait_for(dyo.at[c], rx.at[1])
    send(dyo.at[c], dyo.at[c], ss.at[11], rc.at[1], mate)

    def last(at, carry):
        for row in range(4):
            ref = wqo.at[at, row, 1 - xh, pl.ds(27 * (1 - xl), 27)]
            wait_for(ref, rs.at[0, lax.rem(at + 8 - z, 8), row])

            @pl.when(lax.div(at, 4) == c)
            def _():
                ref = wpo.at[lax.rem(at, 4), row, 1 - xh, pl.ds(9 * (1 - xl), 9)]
                wait_for(ref, rs.at[1, lax.rem(at + 8 - z, 8), row])

        return carry

    lax.fori_loop(0, 8, last, 0)
    wait_for(xo.at[1 - c], rc.at[0])
    wait_for(dyo.at[1 - c], rc.at[1])

    wait_for(wqo.at[pl.ds(0, 7), 0, 0], ss.at[0])
    z_sends = (0, 7, 6, 0, 1, 2)
    for j in z_sends:
        @pl.when(lax.div(lax.rem(z + j, 8), 4) == c)
        def _():
            wait_for(wp_ref, ss.at[1])
    for j, core in ((5, 0), (3, 1)):
        @pl.when(jnp.logical_and(c == core, lax.div(lax.rem(z + j, 8), 4) == c))
        def _():
            wait_for(wp_ref, ss.at[1])
    wait_for(xo.at[0, pl.ds(0, 63)], ss.at[2])
    wait_for(xo.at[0, pl.ds(0, 63)], ss.at[3])
    wait_for(wqo.at[:, pl.ds(0, 3), 0], ss.at[4])
    wait_for(wpo.at[:, pl.ds(0, 3), 0], ss.at[5])
    for sem in (6, 8):
        wait_for(wqo.at[:, :, 0, pl.ds(0, 27)], ss.at[sem])
    for sem in (7, 9):
        wait_for(wpo.at[:, :, 0, pl.ds(0, 9)], ss.at[sem])
    wait_for(xo.at[0], ss.at[10])
    wait_for(xo.at[0], ss.at[11])


def bring(x, dy, wq, wp):
    dma = pltpu.SemaphoreType.DMA
    anywhere = pl.BlockSpec(memory_space=pl.ANY)
    return pl.pallas_call(
        bring_kernel,
        out_shape=(
            jax.ShapeDtypeStruct((2, 64, 9, 2, LANES), F32),
            jax.ShapeDtypeStruct((2, 64, 9, 2, LANES), F32),
            jax.ShapeDtypeStruct((8, 4, 2, 54, 2, LANES), F32),
            jax.ShapeDtypeStruct((4, 4, 2, 18, 4, LANES), F32),
        ),
        in_specs=[anywhere] * 4,
        out_specs=(anywhere,) * 4,
        scratch_shapes=[
            dma((12,)), dma((2,)), dma((2, 8)), dma((2, 8, 4)), dma((2, 8, 4)), dma((2, 8, 4)), dma((2,)),
        ],
        compiler_params=pltpu.CompilerParams(collective_id=0, has_side_effects=True),
    )(x, dy, wq, wp)


def split(v):
    high = v.astype(BF16)
    return high, (v - high.astype(F32)).astype(BF16)


def mm(a, b, ca, cb):
    return lax.dot_general(a, b, (((ca,), (cb,)), ((), ())), preferred_element_type=F32)


def mm3(a, b, ca, cb):
    return mm(a[0], b[0], ca, cb) + (mm(a[1], b[0], ca, cb) + mm(a[0], b[1], ca, cb))


def compute_kernel(
    x_ref, dy_ref, wq_ref, wp_ref, gain_ref, bias_ref,
    out_ref, dx_ref, gq_ref, gp_ref, small_ref,
    xhat, rstd, nh, nl, yh, yl, wh, wl, ph, plo, qkv, da, ah, al, dh, dl,
):
    cols = [slice(LANES * j, LANES * (j + 1)) for j in range(9)]
    gain = gain_ref[...]
    bias = bias_ref[...]
    for j in range(9):
        wh[:, cols[j]], wl[:, cols[j]] = split(wq_ref[pl.ds(j, WIDTH, stride=9), :])
    for j in range(6):
        ph[:, cols[j]], plo[:, cols[j]] = split(wp_ref[pl.ds(j, HALF, stride=6), :])
    dy_sum = jnp.zeros((1, WIDTH), F32)
    for g in range(6):
        base = (g // 3) * 1152 + (g % 3) * 6
        rows = slice(64 * g, 64 * (g + 1))
        x = jnp.concatenate([x_ref[pl.ds(base + j, 64, stride=18), :] for j in range(6)], axis=1)
        centred = x - jnp.mean(x, axis=1, keepdims=True)
        r = lax.rsqrt(jnp.mean(centred * centred, axis=1, keepdims=True) + EPSILON)
        hat = centred * r
        xhat[rows, :] = hat
        rstd[rows, :] = jnp.broadcast_to(r, (64, LANES))
        nh[rows, :], nl[rows, :] = split(hat * gain + bias)
        y = jnp.concatenate([dy_ref[pl.ds(base + j, 64, stride=18), :] for j in range(6)], axis=1)
        yh[rows, :], yl[rows, :] = split(y)
        dy_sum = dy_sum + jnp.sum(y, axis=0, keepdims=True)
    for t in range(3):
        part = slice(HALF * t, HALF * (t + 1))
        qkv[:, part] = mm3((nh[...], nl[...]), (wh[:, part], wl[:, part]), 1, 0)
    da[...] = mm3((yh[...], yl[...]), (ph[...], plo[...]), 1, 1)
    left = lax.broadcasted_iota(jnp.int32, (LANES, LANES), 1) < 64
    row = lax.broadcasted_iota(jnp.int32, (2 * LANES, LANES), 0)
    col = lax.broadcasted_iota(jnp.int32, (2 * LANES, LANES), 1)
    same = ((row % LANES) < 64) == (col < 64)

    def stacked(v):
        return jnp.concatenate([jnp.where(left, v, 0.0), jnp.where(left, 0.0, v)], axis=0)

    def joined(v):
        return jnp.where(left, v[:LANES], v[LANES:])

    scale = 0.125
    for i in range(3):
        rows = slice(LANES * i, LANES * (i + 1))
        for h in range(3):
            q = split(stacked(qkv[rows, cols[h]] * scale))
            k = split(qkv[rows, cols[3 + h]])
            v = split(qkv[rows, cols[6 + h]])
            a = split(stacked(da[rows, cols[h]]))
            scores = jnp.where(same, mm3(q, k, 1, 1), -1e30)
            e = jnp.exp(scores - jnp.max(scores, axis=1, keepdims=True))
            probs = e / jnp.sum(e, axis=1, keepdims=True)
            pair = split(probs)
            ah[rows, cols[h]], al[rows, cols[h]] = split(joined(mm3(pair, v, 1, 0)))
            dh[rows, cols[6 + h]], dl[rows, cols[6 + h]] = split(mm3(pair, a, 0, 0))
            t = mm3(a, v, 1, 1) * probs
            ds = split(t - probs * jnp.sum(t, axis=1, keepdims=True))
            dh[rows, cols[h]], dl[rows, cols[h]] = split(joined(mm3(ds, k, 1, 0)) * scale)
            dh[rows, cols[3 + h]], dl[rows, cols[3 + h]] = split(mm3(ds, q, 0, 0))
    for t in range(2):
        part = slice(HALF * t, HALF * (t + 1))
        o = mm3((ah[...], al[...]), (ph[:, part], plo[:, part]), 1, 0)
        for g in range(6):
            for j in range(3):
                out_ref[pl.ds((g // 3) * 1152 + (g % 3) * 6 + 3 * t + j, 64, stride=18), :] = (
                    o[64 * g : 64 * (g + 1), cols[j]]
                )
        w = mm3((ah[...], al[...]), (yh[:, part], yl[:, part]), 0, 0)
        for j in range(3):
            gp_ref[pl.ds(3 * t + j, HALF, stride=6), :] = w[:, cols[j]]
    for t in range(3):
        part = slice(HALF * t, HALF * (t + 1))
        w = mm3((nh[...], nl[...]), (dh[:, part], dl[:, part]), 0, 0)
        for j in range(3):
            gq_ref[pl.ds(3 * t + j, WIDTH, stride=9), :] = w[:, cols[j]]
    gain_sum = jnp.zeros((1, WIDTH), F32)
    bias_sum = jnp.zeros((1, WIDTH), F32)
    for i in range(3):
        dn = mm3((dh[128 * i : 128 * (i + 1), :], dl[128 * i : 128 * (i + 1), :]), (wh[...], wl[...]), 1, 1)
        for half in range(2):
            g = 2 * i + half
            rows = slice(64 * g, 64 * (g + 1))
            n = dn[64 * half : 64 * (half + 1)]
            hat = xhat[rows, :]
            gain_sum = gain_sum + jnp.sum(n * hat, axis=0, keepdims=True)
            bias_sum = bias_sum + jnp.sum(n, axis=0, keepdims=True)
            n = n * gain
            m1 = jnp.mean(n, axis=1, keepdims=True)
            m2 = jnp.mean(n * hat, axis=1, keepdims=True)
            r = rstd[rows, 0:1]
            dx = r * (n - m1 - hat * m2)
            for j in range(6):
                dx_ref[pl.ds((g // 3) * 1152 + (g % 3) * 6 + j, 64, stride=18), :] = dx[:, cols[j]]
    for n, v in enumerate((gain_sum, bias_sum, dy_sum * 0.5)):
        for j in range(6):
            small_ref[6 * n + j : 6 * n + j + 1, :] = v[:, cols[j]]
    small_ref[18:24, :] = jnp.zeros((6, LANES), F32)


def compute(x, dy, wq, wp, gain, bias):
    vmem = pl.BlockSpec(memory_space=pltpu.VMEM)
    tokens = HALF
    return pl.pallas_call(
        compute_kernel,
        out_shape=(
            jax.ShapeDtypeStruct((2304, LANES), F32),
            jax.ShapeDtypeStruct((2304, LANES), F32),
            jax.ShapeDtypeStruct((6912, LANES), F32),
            jax.ShapeDtypeStruct((2304, LANES), F32),
            jax.ShapeDtypeStruct((24, LANES), F32),
        ),
        in_specs=[vmem] * 6,
        out_specs=(vmem,) * 5,
        scratch_shapes=[
            pltpu.VMEM((tokens, WIDTH), F32),
            pltpu.VMEM((tokens, LANES), F32),
            pltpu.VMEM((tokens, WIDTH), BF16),
            pltpu.VMEM((tokens, WIDTH), BF16),
            pltpu.VMEM((tokens, WIDTH), BF16),
            pltpu.VMEM((tokens, WIDTH), BF16),
            pltpu.VMEM((WIDTH, 3 * HALF), BF16),
            pltpu.VMEM((WIDTH, 3 * HALF), BF16),
            pltpu.VMEM((HALF, WIDTH), BF16),
            pltpu.VMEM((HALF, WIDTH), BF16),
            pltpu.VMEM((tokens, 3 * HALF), F32),
            pltpu.VMEM((tokens, HALF), F32),
            pltpu.VMEM((tokens, HALF), BF16),
            pltpu.VMEM((tokens, HALF), BF16),
            pltpu.VMEM((tokens, 3 * HALF), BF16),
            pltpu.VMEM((tokens, 3 * HALF), BF16),
        ],
        compiler_params=pltpu.CompilerParams(vmem_limit_bytes=50 * 1024 * 1024),
    )(x, dy, wq, wp, gain, bias)


RORDER = (4, 5, 3, 6, 2, 7, 1, 0)


def give_kernel(
    o_ref, dx_ref, gq_ref, gp_ref, sm_ref, of, df, rq, rp, so,
    ob, db, r1q, r1p, r2q, r2p, aq, ap, hq, hp, fq, fp, zq, zp, eq, ep, es, smx, smy, smz,
    ss, rb, r1, r2, rh, rf, rz, ro, ra, re,
):
    s, d, z, y, xh, xl, c = position()
    mirror, side, mate = others(s, d, xh, xl, c)
    corner = device(s, (1 - xl) * 2 + 1 - c)
    greet(s, d, z, y, xh, xl, c, corner)
    holds = lax.div(z, 4) == c
    oxh = 1 - xh
    mine_q, mine_p = pl.ds(27 * xl, 27), pl.ds(9 * xl, 9)
    yours_q, yours_p = pl.ds(27 * (1 - xl), 27), pl.ds(9 * (1 - xl), 9)

    def zdev(k):
        return device((lax.rem(z + k + 8, 8) * 4 + y) * 2 + xh, d)

    def ydev(k):
        return device((z * 4 + lax.rem(y + k, 4)) * 2 + xh, d)

    def row(k):
        return lax.rem(y + k, 4)

    def both(j, q_job, p_job):
        at = lax.rem(z + j, 8)
        q_job(at)

        @pl.when(lax.div(at, 4) == c)
        def _():
            p_job(lax.rem(at, 4))

    ROWS = (2, 1, 3, 0)

    def side_send(j):
        for k in ROWS:
            both(
                j,
                lambda at: send(gq_ref.at[at, row(k), oxh, yours_q], r1q.at[j, k], ss.at[0], r1.at[0, j, k], side),
                lambda at: send(gp_ref.at[at, row(k), oxh, yours_p], r1p.at[j, k], ss.at[1], r1.at[1, j, k], side),
            )

    def mirror_send(j):
        for k in ROWS:
            def q(at):
                wait_for(r1q.at[j, k], r1.at[0, j, k])
                r1q[j, k] = r1q[j, k] + gq_ref[at, row(k), oxh, mine_q]
                send(r1q.at[j, k], r2q.at[j, k], ss.at[5], r2.at[0, j, k], mirror)

            def p(at):
                wait_for(r1p.at[j, k], r1.at[1, j, k])
                r1p[j, k] = r1p[j, k] + gp_ref[at, row(k), oxh, mine_p]
                send(r1p.at[j, k], r2p.at[j, k], ss.at[6], r2.at[1, j, k], mirror)

            both(j, q, p)

    def gather(j, k):
        def q(at):
            wait_for(r2q.at[j, k], r2.at[0, j, k])
            aq[j, k, mine_q] = gq_ref[at, row(k), xh, mine_q]
            aq[j, k, yours_q] = gq_ref[at, row(k), xh, yours_q] + r2q[j, k]

        def p(at):
            wait_for(r2p.at[j, k], r2.at[1, j, k])
            ap[j, k, mine_p] = gp_ref[at, row(k), xh, mine_p]
            ap[j, k, yours_p] = gp_ref[at, row(k), xh, yours_p] + r2p[j, k]

        both(j, q, p)

    def y_far(j):
        gather(j, 2)
        for n, k in ((0, 1), (1, 3)):
            both(
                j,
                lambda at: send(aq.at[j, 2, pl.ds(27 * n, 27)], hq.at[j, n], ss.at[10], rh.at[0, j, n], ydev(k)),
                lambda at: send(ap.at[j, 2, pl.ds(9 * n, 9)], hp.at[j, n], ss.at[11], rh.at[1, j, n], ydev(k)),
            )

    def y_near(j):
        for n, k in ((0, 1), (1, 3)):
            gather(j, k)

            def q(at):
                wait_for(hq.at[j, n], rh.at[0, j, n])
                part = pl.ds(27 * n, 27)
                aq[j, k, part] = aq[j, k, part] + hq[j, n]
                send(aq.at[j, k], fq.at[j, n], ss.at[10], rf.at[0, j, n], ydev(k))

            def p(at):
                wait_for(hp.at[j, n], rh.at[1, j, n])
                part = pl.ds(9 * n, 9)
                ap[j, k, part] = ap[j, k, part] + hp[j, n]
                send(ap.at[j, k], fp.at[j, n], ss.at[11], rf.at[1, j, n], ydev(k))

            both(j, q, p)

    def z_step(j):
        gather(j, 0)

        def q(at):
            wait_for(fq.at[j, 0], rf.at[0, j, 0])
            wait_for(fq.at[j, 1], rf.at[0, j, 1])
            aq[j, 0] = aq[j, 0] + (fq[j, 0] + fq[j, 1])

        def p(at):
            wait_for(fp.at[j, 0], rf.at[1, j, 0])
            wait_for(fp.at[j, 1], rf.at[1, j, 1])
            ap[j, 0] = ap[j, 0] + (fp[j, 0] + fp[j, 1])

        both(j, q, p)

        def come(slot):
            def q(at):
                wait_for(zq.at[slot], rz.at[0, slot])
                aq[j, 0] = aq[j, 0] + zq[slot]

            def p(at):
                wait_for(zp.at[slot], rz.at[1, slot])
                ap[j, 0] = ap[j, 0] + zp[slot]

            both(j, q, p)

        def go(slot, k):
            both(
                j,
                lambda at: send(aq.at[j, 0], zq.at[slot], ss.at[13], rz.at[0, slot], zdev(k)),
                lambda at: send(ap.at[j, 0], zp.at[slot], ss.at[14], rz.at[1, slot], zdev(k)),
            )

        if j == 4:
            @pl.when(c == 0)
            def _():
                go(3, 1)

            @pl.when(c == 1)
            def _():
                go(5, -1)
        elif j == 0:
            come(0)
            come(8)
        else:
            if j in (3, 5):
                @pl.when(c == (0 if j == 3 else 1))
                def _():
                    come(j)
            else:
                come(j)
            if j < 4:
                go(j - 1, 1)
            else:
                go(j + 1, -1)

    def joined(n):
        own, buf, out = ((o_ref, ob, of), (dx_ref, db, df))[n]
        wait_for(buf, rb.at[n])

        def add(i, carry):
            at = pl.ds(8 * i, 8)
            buf[at] = buf[at] + own[c, at]
            return carry

        lax.fori_loop(0, 8, add, 0)
        pltpu.make_async_copy(buf.at[s], out.at[s], ro.at[n]).start()

    def spread(n, first, last):
        buf, out = ((ob, of), (db, df))[n]

        def one(k, carry):
            t = lax.rem(s + k, 64)
            send(buf.at[t], out.at[s], ss.at[7 + n], ro.at[n], device(t, d))
            return carry

        lax.fori_loop(first, last, one, 0)

    def small(step):
        if step == 0:
            smx[0] = sm_ref[...]
            send(smx.at[0], smx.at[1], ss.at[4], ra.at[0], mirror)
        if step == 1:
            wait_for(smx.at[1], ra.at[0])
            smy[y] = smx[0] + smx[1]
            for k in range(1, 4):
                send(smy.at[y], smy.at[y], ss.at[9], ra.at[1], ydev(k))
        if step == 2:
            wait_for(smy.at[pl.ds(0, 3)], ra.at[1])
            smz[z] = (smy[0] + smy[1]) + (smy[2] + smy[3])
            for k in range(1, 8):
                send(smz.at[z], smz.at[z], ss.at[12], ra.at[2], zdev(k))
        if step == 3:
            wait_for(smz.at[pl.ds(0, 7)], ra.at[2])
            es[d] = ((smz[0] + smz[1]) + (smz[2] + smz[3])) + ((smz[4] + smz[5]) + (smz[6] + smz[7]))
            for there in (side, mate, corner):
                send(es.at[d], es.at[d], ss.at[17], re.at[2], there)

    side_send(RORDER[0])
    send(o_ref.at[1 - c], ob, ss.at[2], rb.at[0], mate)
    send(dx_ref.at[1 - c], db, ss.at[3], rb.at[1], mate)
    side_send(RORDER[1])
    small(0)
    for t in range(1, 13):
        if t + 1 < 8:
            side_send(RORDER[t + 1])
        if 1 <= t < 9:
            mirror_send(RORDER[t - 1])
        if 2 <= t < 10:
            y_far(RORDER[t - 2])
        if 3 <= t < 11:
            y_near(RORDER[t - 3])
        if 4 <= t < 12:
            z_step(RORDER[t - 4])
        if t in (2, 4, 6):
            small(t // 2)
        if t == 1:
            joined(0)
        if t == 1:
            spread(0, 1, 17)
        if t == 2:
            spread(0, 17, 33)
        if t == 3:
            spread(0, 33, 49)
        if t == 4:
            spread(0, 49, 64)
        if t == 5:
            joined(1)
        if t == 5:
            spread(1, 1, 17)
        if t == 6:
            spread(1, 17, 33)
        if t == 7:
            spread(1, 33, 49)
        if t == 8:
            spread(1, 49, 64)

    eq[d] = aq[0, 0]
    for there in (side, mate, corner):
        send(eq.at[d], eq.at[d], ss.at[15], re.at[0], there)

    @pl.when(holds)
    def _():
        ep[xl] = ap[0, 0]
        for there in (side, mate, corner):
            send(ep.at[xl], ep.at[xl], ss.at[16], re.at[1], there)

    wait_for(es.at[pl.ds(0, 3)], re.at[2])
    so[...] = (es[0] + es[2]) + (es[1] + es[3])
    wait_for(eq.at[pl.ds(0, 3)], re.at[0])
    rq[0] = eq[0] + eq[2]
    rq[1] = eq[1] + eq[3]

    @pl.when(holds)
    def _():
        wait_for(ep.at[0], re.at[1])

    @pl.when(jnp.logical_not(holds))
    def _():
        wait_for(ep, re.at[1])

    rp[...] = ep[0] + ep[1]

    wait_for(ob, ro.at[0])
    wait_for(db, ro.at[1])
    wait_for(r1q, ss.at[0])
    wait_for(r1p.at[pl.ds(0, 4)], ss.at[1])
    wait_for(ob, ss.at[2])
    wait_for(db, ss.at[3])
    wait_for(smx.at[0], ss.at[4])
    wait_for(r2q, ss.at[5])
    wait_for(r2p.at[pl.ds(0, 4)], ss.at[6])
    wait_for(ob.at[pl.ds(0, 63)], ss.at[7])
    wait_for(db.at[pl.ds(0, 63)], ss.at[8])
    wait_for(smy.at[pl.ds(0, 3)], ss.at[9])
    wait_for(aq.at[:, pl.ds(0, 3)], ss.at[10])
    wait_for(ap.at[pl.ds(0, 4), pl.ds(0, 3)], ss.at[11])
    wait_for(smz.at[pl.ds(0, 7)], ss.at[12])
    wait_for(zq.at[pl.ds(0, 7)], ss.at[13])
    wait_for(eq.at[pl.ds(0, 3)], ss.at[15])
    wait_for(es.at[pl.ds(0, 3)], ss.at[17])

    @pl.when(holds)
    def _():
        wait_for(zp.at[pl.ds(0, 3)], ss.at[14])
        wait_for(zp.at[pl.ds(0, 3)], ss.at[16])

    @pl.when(jnp.logical_not(holds))
    def _():
        wait_for(zp.at[pl.ds(0, 4)], ss.at[14])


def give(o, dx, gq, gp, sm):
    dma = pltpu.SemaphoreType.DMA
    anywhere = pl.BlockSpec(memory_space=pl.ANY)
    vmem = pl.BlockSpec(memory_space=pltpu.VMEM)
    act = (64, 9, 2, LANES)
    q, p, sml = (54, 2, LANES), (18, 4, LANES), (24, LANES)
    q2, p2 = (27, 2, LANES), (9, 4, LANES)

    def buf(*shape):
        return pltpu.VMEM(shape, F32)

    return pl.pallas_call(
        give_kernel,
        out_shape=(
            jax.ShapeDtypeStruct(act, F32),
            jax.ShapeDtypeStruct(act, F32),
            jax.ShapeDtypeStruct((2,) + q, F32),
            jax.ShapeDtypeStruct(p, F32),
            jax.ShapeDtypeStruct(sml, F32),
        ),
        in_specs=[vmem] * 5,
        out_specs=(anywhere, anywhere, vmem, vmem, vmem),
        scratch_shapes=[
            buf(*act), buf(*act),
            buf(8, 4, *q2), buf(8, 4, *p2), buf(8, 4, *q2), buf(8, 4, *p2),
            buf(8, 4, *q), buf(8, 4, *p), buf(8, 2, *q2), buf(8, 2, *p2), buf(8, 2, *q), buf(8, 2, *p),
            buf(9, *q), buf(9, *p), buf(4, *q), buf(2, *p), buf(4, *sml),
            buf(2, *sml), buf(4, *sml), buf(8, *sml),
            dma((18,)), dma((2,)), dma((2, 8, 4)), dma((2, 8, 4)), dma((2, 8, 2)), dma((2, 8, 2)), dma((2, 9)),
            dma((2,)), dma((3,)), dma((3,)),
        ],
        compiler_params=pltpu.CompilerParams(
            collective_id=1, has_side_effects=True, vmem_limit_bytes=50 * 1024 * 1024
        ),
    )(o, dx, gq, gp, sm)


def on_device(
    frames, out_cotangent, layer_norm_gain, layer_norm_bias, qkv_weight, proj_weight, proj_bias
):
    c = lax.rem(lax.axis_index("dp"), 2)
    blocks = (64, 9, 2, LANES)
    half = lax.dynamic_index_in_dim(qkv_weight.reshape(12, 3, 2, HALF), c, axis=2, keepdims=False)
    x, dy, wq, wp = bring(
        frames.reshape(blocks),
        out_cotangent.reshape(blocks),
        half.reshape(54, 2, LANES),
        proj_weight.reshape(18, 4, LANES),
    )
    o, dx, gq, gp, small = compute(
        x.reshape(2304, LANES),
        dy.reshape(2304, LANES),
        wq.reshape(6912, LANES),
        wp.reshape(2304, LANES),
        layer_norm_gain.reshape(1, WIDTH),
        layer_norm_bias.reshape(1, WIDTH),
    )
    of, df, rq, rp, so = give(
        o.reshape((2,) + blocks),
        dx.reshape((2,) + blocks),
        gq.reshape(8, 4, 2, 54, 2, LANES),
        gp.reshape(4, 4, 2, 18, 4, LANES),
        small,
    )
    sums = so[:18].reshape(3, WIDTH)
    grad_qkv = jnp.transpose(rq.reshape(2, 12, 3, HALF), (1, 2, 0, 3)).reshape(12, 3 * WIDTH)
    return (
        frames + of.reshape(frames.shape) + proj_bias,
        out_cotangent + df.reshape(frames.shape),
        sums[0],
        sums[1],
        grad_qkv,
        rp.reshape(12, WIDTH),
        sums[2],
    )


def solution(mesh):
    return jax.shard_map(
        on_device,
        mesh=mesh,
        in_specs=(
            P("dp", "seq", None, None),
            P("dp", "seq", None, None),
            P(),
            P(),
            P("seq", None),
            P("seq", None),
            P(),
        ),
        out_specs=(
            P("dp", "seq", None, None),
            P("dp", "seq", None, None),
            P(),
            P(),
            P("seq", None),
            P("seq", None),
            P(),
        ),
        check_vma=False,
    )
```

```python
import jax
import jax.numpy as jnp
from jax import lax
from jax.experimental import pallas as pl
from jax.experimental.pallas import tpu as pltpu
from jax.sharding import PartitionSpec as P

EPSILON = 1e-06
MESH = pl.DeviceIdType.MESH
F32 = jnp.float32
BF16 = jnp.bfloat16
WIDTH = 768
HALF = 384
LANES = 128


def position():
    s = lax.axis_index("seq")
    d = lax.axis_index("dp")
    return s, d, lax.div(s, 8), lax.rem(lax.div(s, 2), 4), lax.rem(s, 2), lax.div(d, 2), lax.rem(d, 2)


def device(s, d):
    return {"seq": s, "dp": d}


def greet(s, d, near):
    barrier = pltpu.get_barrier_semaphore()

    def one(k, carry):
        pl.semaphore_signal(barrier, inc=1, device_id=device(lax.rem(s + k, 64), d), device_id_type=MESH)
        return carry

    lax.fori_loop(1, 64, one, 0)
    for where in near:
        pl.semaphore_signal(barrier, inc=1, device_id=where, device_id_type=MESH)


def others(s, d, xh, xl, c):
    mirror = device(s + 1 - 2 * xh, (1 - xl) * 2 + c)
    side = device(s, (1 - xl) * 2 + c)
    mate = device(s, xl * 2 + 1 - c)
    return mirror, side, mate


def send(src, dst, send_sem, recv_sem, where):
    copy = pltpu.make_async_remote_copy(
        src_ref=src, dst_ref=dst, send_sem=send_sem, recv_sem=recv_sem, device_id=where, device_id_type=MESH
    )
    copy.start()


def wait_for(ref, sem):
    pltpu.make_async_copy(ref, ref, sem).wait()


def split(v):
    high = v.astype(BF16)
    return high, (v - high.astype(F32)).astype(BF16)


def mm(a, b, ca, cb):
    return lax.dot_general(a, b, (((ca,), (cb,)), ((), ())), preferred_element_type=F32)


def mm3(a, b, ca, cb):
    return mm(a[0], b[0], ca, cb) + (mm(a[1], b[0], ca, cb) + mm(a[0], b[1], ca, cb))


def stacked(left, v):
    return jnp.concatenate([jnp.where(left, v, 0.0), jnp.where(left, 0.0, v)], axis=0)


def joined_heads(left, v):
    return jnp.where(left, v[:LANES], v[LANES:])


ORDER = (0, 1, 7, 2, 6, 3, 5, 4)
RORDER = (4, 5, 3, 6, 2, 7, 1, 0)
ROWS = (2, 1, 3, 0)
COLS = [slice(LANES * j, LANES * (j + 1)) for j in range(9)]


def layer_kernel(
    x_ref, dy_ref, wq_raw, wp_raw, vec_ref, of, df, rq, rp, so,
    wq_own, wp_own, x2, dy2, wq2, wp2,
    xhat, rstd, nh, nl, yh, yl, wh, wl, ph, plo, qkv, da, ah, al, dh, dl, o2, d2, gq2, gp2, sm,
    ob, db, r1q, r1p, r2q, r2p, aq, ap, hq, hp, fq, fp, zq, zp, eq, ep, es, smx, smy, smz,
    ss, rx, rz, ry, rm, rs, rc, so_sem, rb, r1s, r2s, rh, rf, rzz, ro, ra, re,
):
    s, d, z, y, xh, xl, c = position()
    mirror, side, mate = others(s, d, xh, xl, c)
    corner = device(s, (1 - xl) * 2 + 1 - c)
    greet(s, d, (mirror, side, mate, corner))
    holds = lax.div(z, 4) == c
    for t in range(3):
        for n in range(3):
            at = pl.multiple_of(WIDTH * t + HALF * c + LANES * n, LANES)
            wq_own[pl.ds(3 * t + n, 12, stride=9), :] = wq_raw[:, pl.ds(at, LANES)]
    for n in range(6):
        wp_own[pl.ds(n, 12, stride=6), :] = wp_raw[:, COLS[n]]
    sm[...] = jnp.zeros((24, LANES), F32)
    wq_ref, wp_ref = wq_own.reshape(54, 2, LANES), wp_own.reshape(18, 4, LANES)
    xo, dyo = x2.reshape(2, 64, 9, 2, LANES), dy2.reshape(2, 64, 9, 2, LANES)
    o_ref, dx_ref = o2.reshape(2, 64, 9, 2, LANES), d2.reshape(2, 64, 9, 2, LANES)
    wqo, wpo = wq2.reshape(8, 4, 2, 54, 2, LANES), wp2.reshape(4, 4, 2, 18, 4, LANES)
    gq_ref, gp_ref = gq2.reshape(8, 4, 2, 54, 2, LANES), gp2.reshape(4, 4, 2, 18, 4, LANES)
    pl.semaphore_wait(pltpu.get_barrier_semaphore(), 67)

    def zdev(k):
        return device((lax.rem(z + k + 8, 8) * 4 + y) * 2 + xh, d)

    def ydev(k):
        return device((z * 4 + lax.rem(y + k, 4)) * 2 + xh, d)

    def both(j, q_job, p_job):
        at = lax.rem(z + j, 8)
        q_job(at)

        @pl.when(lax.div(at, 4) == c)
        def _():
            p_job(lax.rem(at, 4))

    def along_z(j, to, there, src_q=None, src_p=None):
        both(
            j,
            lambda at: send(wqo.at[at, y, xh] if src_q is None else src_q, wqo.at[at, y, xh], ss.at[0], rz.at[0, to], there),
            lambda at: send(wpo.at[at, y, xh] if src_p is None else src_p, wpo.at[at, y, xh], ss.at[1], rz.at[1, to], there),
        )

    def z_stage(j):
        if j == 0:
            along_z(0, 7, zdev(1), wq_ref, wp_ref)
            along_z(0, 1, zdev(-1), wq_ref, wp_ref)
            both(
                0,
                lambda at: pltpu.make_async_copy(wq_ref, wqo.at[at, y, xh], rz.at[0, 0]).start(),
                lambda at: pltpu.make_async_copy(wp_ref, wpo.at[at, y, xh], rz.at[1, 0]).start(),
            )
        both(
            j,
            lambda at: wait_for(wqo.at[at, y, xh], rz.at[0, j]),
            lambda at: wait_for(wpo.at[at, y, xh], rz.at[1, j]),
        )
        if j in (7, 6):
            along_z(j, j - 1, zdev(1))
        if j in (1, 2):
            along_z(j, j + 1, zdev(-1))
        if j == 5:
            @pl.when(c == 0)
            def _():
                along_z(5, 4, zdev(1))
        if j == 3:
            @pl.when(c == 1)
            def _():
                along_z(3, 4, zdev(-1))

    def y_send(j):
        for k in (1, 3):
            both(
                j,
                lambda at: send(wqo.at[at, y, xh], wqo.at[at, y, xh], ss.at[4], ry.at[0, j, k], ydev(k)),
                lambda at: send(wpo.at[at, y, xh], wpo.at[at, y, xh], ss.at[5], ry.at[1, j, k], ydev(k)),
            )

    def across(j, k):
        row = lax.rem(y + 4 - k, 4)
        hq, hp = pl.ds(27 * (1 - xl), 27), pl.ds(9 * (1 - xl), 9)

        def q(at):
            ref = wqo.at[at, row, xh, hq]
            send(ref, ref, ss.at[6], rm.at[0, j, row], mirror)

        def p(at):
            ref = wpo.at[at, row, xh, hp]
            send(ref, ref, ss.at[7], rm.at[1, j, row], mirror)

        both(j, q, p)

    def y_wait(j, k):
        row = lax.rem(y + 4 - k, 4)
        both(
            j,
            lambda at: wait_for(wqo.at[at, row, xh], ry.at[0, j, k]),
            lambda at: wait_for(wpo.at[at, row, xh], ry.at[1, j, k]),
        )

    def y_pass(j, k):
        h = 0 if k == 1 else 1
        row = lax.rem(y + 4 - k, 4)

        def q(at):
            ref = wqo.at[at, row, xh, pl.ds(27 * h, 27)]
            send(ref, ref, ss.at[4], ry.at[0, j, 2], ydev(k))

        def p(at):
            ref = wpo.at[at, row, xh, pl.ds(9 * h, 9)]
            send(ref, ref, ss.at[5], ry.at[1, j, 2], ydev(k))

        both(j, q, p)

    def forward(j, k):
        row = lax.rem(y + 4 - k, 4)
        hq, hp = pl.ds(27 * xl, 27), pl.ds(9 * xl, 9)

        def q(at):
            ref = wqo.at[at, row, 1 - xh, hq]
            wait_for(ref, rm.at[0, j, row])
            send(ref, ref, ss.at[8], rs.at[0, j, row], side)

        def p(at):
            ref = wpo.at[at, row, 1 - xh, hp]
            wait_for(ref, rm.at[1, j, row])
            send(ref, ref, ss.at[9], rs.at[1, j, row], side)

        both(j, q, p)

    pltpu.make_async_copy(x_ref.at[s], xo.at[c, s], rx.at[0]).start()
    pltpu.make_async_copy(dy_ref.at[s], dyo.at[c, s], rx.at[1]).start()

    def spread_in(n, first, last):
        src, dst = ((x_ref, xo), (dy_ref, dyo))[n]

        def one(k, carry):
            t = lax.rem(s + k, 64)
            send(src.at[t], dst.at[c, s], ss.at[2 + n], rx.at[n], device(t, d))
            return carry

        lax.fori_loop(first, last, one, 0)

    gain = vec_ref[0:1, :]
    bias = vec_ref[1:2, :]

    def weights(j):
        at = lax.rem(z + j, 8)
        for k in range(4):
            row = lax.rem(y + 4 - k, 4)
            both(
                j,
                lambda at: wait_for(wqo.at[at, row, 1 - xh, pl.ds(27 * (1 - xl), 27)], rs.at[0, j, row]),
                lambda at: wait_for(wpo.at[at, row, 1 - xh, pl.ds(9 * (1 - xl), 9)], rs.at[1, j, row]),
            )

        def q(at):
            rows = pl.ds(pl.multiple_of(at * 96, 96), 96)
            for n in range(9):
                wh[rows, COLS[n]], wl[rows, COLS[n]] = split(wq2[pl.ds(at * 864 + n, 96, stride=9), :])

        def p(at):
            rows = pl.ds(pl.multiple_of(at * 96, 96), 96)
            for n in range(6):
                ph[rows, COLS[n]], plo[rows, COLS[n]] = split(wp2[pl.ds(at * 576 + n, 96, stride=6), :])

        both(j, q, p)

    def tokens(ref, g):
        base = (g // 3) * 1152 + (g % 3) * 6
        return jnp.concatenate([ref[pl.ds(base + n, 64, stride=18), :] for n in range(6)], axis=1)

    def norm(g):
        rows = slice(64 * g, 64 * (g + 1))
        v = tokens(x2, g)
        centred = v - jnp.mean(v, axis=1, keepdims=True)
        r = lax.rsqrt(jnp.mean(centred * centred, axis=1, keepdims=True) + EPSILON)
        hat = centred * r
        xhat[rows, :] = hat
        rstd[rows, :] = jnp.broadcast_to(r, (64, LANES))
        nh[rows, :], nl[rows, :] = split(hat * gain + bias)

    def cotangent(g):
        rows = slice(64 * g, 64 * (g + 1))
        v = tokens(dy2, g)
        yh[rows, :], yl[rows, :] = split(v)
        add_small(12, jnp.sum(v, axis=0, keepdims=True) * 0.5)

    def add_small(first, v):
        for n in range(6):
            at = slice(first + n, first + n + 1)
            sm[at, :] = sm[at, :] + v[:, COLS[n]]

    def attention():
        left = lax.broadcasted_iota(jnp.int32, (LANES, LANES), 1) < 64
        row = lax.broadcasted_iota(jnp.int32, (2 * LANES, LANES), 0)
        col = lax.broadcasted_iota(jnp.int32, (2 * LANES, LANES), 1)
        same = ((row % LANES) < 64) == (col < 64)
        scale = 0.125
        for i in range(3):
            rows = slice(LANES * i, LANES * (i + 1))
            for h in range(3):
                q = split(stacked(left, qkv[rows, COLS[h]] * scale))
                k = split(qkv[rows, COLS[3 + h]])
                v = split(qkv[rows, COLS[6 + h]])
                a = split(stacked(left, da[rows, COLS[h]]))
                scores = jnp.where(same, mm3(q, k, 1, 1), -1e30)
                e = jnp.exp(scores - jnp.max(scores, axis=1, keepdims=True))
                probs = e / jnp.sum(e, axis=1, keepdims=True)
                pair = split(probs)
                ah[rows, COLS[h]], al[rows, COLS[h]] = split(joined_heads(left, mm3(pair, v, 1, 0)))
                dh[rows, COLS[6 + h]], dl[rows, COLS[6 + h]] = split(mm3(pair, a, 0, 0))
                t = mm3(a, v, 1, 1) * probs
                ds = split(t - probs * jnp.sum(t, axis=1, keepdims=True))
                dh[rows, COLS[h]], dl[rows, COLS[h]] = split(joined_heads(left, mm3(ds, k, 1, 0)) * scale)
                dh[rows, COLS[3 + h]], dl[rows, COLS[3 + h]] = split(mm3(ds, q, 0, 0))

    def project(t):
        part = slice(HALF * t, HALF * (t + 1))
        o = mm3((ah[...], al[...]), (ph[:, part], plo[:, part]), 1, 0)
        for g in range(6):
            for n in range(3):
                o2[pl.ds((g // 3) * 1152 + (g % 3) * 6 + 3 * t + n, 64, stride=18), :] = (
                    o[64 * g : 64 * (g + 1), COLS[n]]
                )

    def grad_proj(t):
        part = slice(HALF * t, HALF * (t + 1))
        w = mm3((ah[...], al[...]), (yh[:, part], yl[:, part]), 0, 0)
        for n in range(3):
            gp2[pl.ds(3 * t + n, HALF, stride=6), :] = w[:, COLS[n]]

    def grad_qkv(t):
        part = slice(HALF * t, HALF * (t + 1))
        w = mm3((nh[...], nl[...]), (dh[:, part], dl[:, part]), 0, 0)
        for n in range(3):
            gq2[pl.ds(3 * t + n, WIDTH, stride=9), :] = w[:, COLS[n]]

    def grad_input(i):
        dn = mm3((dh[128 * i : 128 * (i + 1), :], dl[128 * i : 128 * (i + 1), :]), (wh[...], wl[...]), 1, 1)
        for half in range(2):
            g = 2 * i + half
            rows = slice(64 * g, 64 * (g + 1))
            n = dn[64 * half : 64 * (half + 1)]
            hat = xhat[rows, :]
            add_small(0, jnp.sum(n * hat, axis=0, keepdims=True))
            add_small(6, jnp.sum(n, axis=0, keepdims=True))
            n = n * gain
            m1 = jnp.mean(n, axis=1, keepdims=True)
            m2 = jnp.mean(n * hat, axis=1, keepdims=True)
            dx = rstd[rows, 0:1] * (n - m1 - hat * m2)
            for j in range(6):
                d2[pl.ds((g // 3) * 1152 + (g % 3) * 6 + j, 64, stride=18), :] = dx[:, COLS[j]]

    oxh = 1 - xh
    mine_q, mine_p = pl.ds(27 * xl, 27), pl.ds(9 * xl, 9)
    yours_q, yours_p = pl.ds(27 * (1 - xl), 27), pl.ds(9 * (1 - xl), 9)

    def row(k):
        return lax.rem(y + k, 4)

    def side_send(j):
        for k in ROWS:
            both(
                j,
                lambda at: send(gq_ref.at[at, row(k), oxh, yours_q], r1q.at[j, k], so_sem.at[0], r1s.at[0, j, k], side),
                lambda at: send(gp_ref.at[at, row(k), oxh, yours_p], r1p.at[j, k], so_sem.at[1], r1s.at[1, j, k], side),
            )

    def mirror_send(j):
        for k in ROWS:
            def q(at):
                wait_for(r1q.at[j, k], r1s.at[0, j, k])
                r1q[j, k] = r1q[j, k] + gq_ref[at, row(k), oxh, mine_q]
                send(r1q.at[j, k], r2q.at[j, k], so_sem.at[5], r2s.at[0, j, k], mirror)

            def p(at):
                wait_for(r1p.at[j, k], r1s.at[1, j, k])
                r1p[j, k] = r1p[j, k] + gp_ref[at, row(k), oxh, mine_p]
                send(r1p.at[j, k], r2p.at[j, k], so_sem.at[6], r2s.at[1, j, k], mirror)

            both(j, q, p)

    def gather(j, k):
        def q(at):
            wait_for(r2q.at[j, k], r2s.at[0, j, k])
            aq[j, k, mine_q] = gq_ref[at, row(k), xh, mine_q]
            aq[j, k, yours_q] = gq_ref[at, row(k), xh, yours_q] + r2q[j, k]

        def p(at):
            wait_for(r2p.at[j, k], r2s.at[1, j, k])
            ap[j, k, mine_p] = gp_ref[at, row(k), xh, mine_p]
            ap[j, k, yours_p] = gp_ref[at, row(k), xh, yours_p] + r2p[j, k]

        both(j, q, p)

    def y_far(j):
        gather(j, 2)
        for n, k in ((0, 1), (1, 3)):
            both(
                j,
                lambda at: send(aq.at[j, 2, pl.ds(27 * n, 27)], hq.at[j, n], so_sem.at[10], rh.at[0, j, n], ydev(k)),
                lambda at: send(ap.at[j, 2, pl.ds(9 * n, 9)], hp.at[j, n], so_sem.at[11], rh.at[1, j, n], ydev(k)),
            )

    def y_near(j):
        for n, k in ((0, 1), (1, 3)):
            gather(j, k)

            def q(at):
                wait_for(hq.at[j, n], rh.at[0, j, n])
                part = pl.ds(27 * n, 27)
                aq[j, k, part] = aq[j, k, part] + hq[j, n]
                send(aq.at[j, k], fq.at[j, n], so_sem.at[10], rf.at[0, j, n], ydev(k))

            def p(at):
                wait_for(hp.at[j, n], rh.at[1, j, n])
                part = pl.ds(9 * n, 9)
                ap[j, k, part] = ap[j, k, part] + hp[j, n]
                send(ap.at[j, k], fp.at[j, n], so_sem.at[11], rf.at[1, j, n], ydev(k))

            both(j, q, p)

    def z_step(j):
        gather(j, 0)

        def q(at):
            wait_for(fq.at[j, 0], rf.at[0, j, 0])
            wait_for(fq.at[j, 1], rf.at[0, j, 1])
            aq[j, 0] = aq[j, 0] + (fq[j, 0] + fq[j, 1])

        def p(at):
            wait_for(fp.at[j, 0], rf.at[1, j, 0])
            wait_for(fp.at[j, 1], rf.at[1, j, 1])
            ap[j, 0] = ap[j, 0] + (fp[j, 0] + fp[j, 1])

        both(j, q, p)

        def come(slot):
            def q(at):
                wait_for(zq.at[slot], rzz.at[0, slot])
                aq[j, 0] = aq[j, 0] + zq[slot]

            def p(at):
                wait_for(zp.at[slot], rzz.at[1, slot])
                ap[j, 0] = ap[j, 0] + zp[slot]

            both(j, q, p)

        def go(slot, k):
            both(
                j,
                lambda at: send(aq.at[j, 0], zq.at[slot], so_sem.at[13], rzz.at[0, slot], zdev(k)),
                lambda at: send(ap.at[j, 0], zp.at[slot], so_sem.at[14], rzz.at[1, slot], zdev(k)),
            )

        if j == 4:
            @pl.when(c == 0)
            def _():
                go(3, 1)

            @pl.when(c == 1)
            def _():
                go(5, -1)
        elif j == 0:
            come(0)
            come(8)
        else:
            if j in (3, 5):
                @pl.when(c == (0 if j == 3 else 1))
                def _():
                    come(j)
            else:
                come(j)
            if j < 4:
                go(j - 1, 1)
            else:
                go(j + 1, -1)

    def joined(n):
        own, buf, out = ((o_ref, ob, of), (dx_ref, db, df))[n]
        wait_for(buf, rb.at[n])

        def add(i, carry):
            at = pl.ds(8 * i, 8)
            buf[at] = buf[at] + own[c, at]
            return carry

        lax.fori_loop(0, 8, add, 0)
        pltpu.make_async_copy(buf.at[s], out.at[s], ro.at[n]).start()

    def spread(n, first, last):
        buf, out = ((ob, of), (db, df))[n]

        def one(k, carry):
            t = lax.rem(s + k, 64)
            send(buf.at[t], out.at[s], so_sem.at[7 + n], ro.at[n], device(t, d))
            return carry

        lax.fori_loop(first, last, one, 0)

    def small(step):
        if step == 0:
            smx[0] = sm[...]
            send(smx.at[0], smx.at[1], so_sem.at[4], ra.at[0], mirror)
        if step == 1:
            wait_for(smx.at[1], ra.at[0])
            smy[y] = smx[0] + smx[1]
            for k in range(1, 4):
                send(smy.at[y], smy.at[y], so_sem.at[9], ra.at[1], ydev(k))
        if step == 2:
            wait_for(smy.at[pl.ds(0, 3)], ra.at[1])
            smz[z] = (smy[0] + smy[1]) + (smy[2] + smy[3])
            for k in range(1, 8):
                send(smz.at[z], smz.at[z], so_sem.at[12], ra.at[2], zdev(k))
        if step == 3:
            wait_for(smz.at[pl.ds(0, 7)], ra.at[2])
            es[d] = ((smz[0] + smz[1]) + (smz[2] + smz[3])) + ((smz[4] + smz[5]) + (smz[6] + smz[7]))
            for there in (side, mate, corner):
                send(es.at[d], es.at[d], so_sem.at[17], re.at[2], there)

    for t in range(14):
        if t < 8:
            z_stage(ORDER[t])
            y_send(ORDER[t])
            across(ORDER[t], 0)
        if 1 <= t < 9:
            j = ORDER[t - 1]
            for k in (1, 3):
                y_wait(j, k)
                y_pass(j, k)
                across(j, k)
        if 2 <= t < 10:
            j = ORDER[t - 2]
            y_wait(j, 2)
            across(j, 2)
            forward(j, 0)
        if 3 <= t < 11:
            j = ORDER[t - 3]
            for k in (1, 3, 2):
                forward(j, k)
        if 1 <= t <= 4:
            spread_in(0, 16 * t - 15, min(64, 16 * t + 1))
        if 5 <= t <= 8:
            spread_in(1, 16 * t - 79, min(64, 16 * t - 63))
        if t == 10:
            wait_for(xo.at[c], rx.at[0])
            send(xo.at[c], xo.at[c], ss.at[10], rc.at[0], mate)
        if t == 11:
            wait_for(dyo.at[c], rx.at[1])
            send(dyo.at[c], dyo.at[c], ss.at[11], rc.at[1], mate)
        if 6 <= t < 14:
            weights(ORDER[t - 6])
        if t == 12:
            wait_for(xo.at[1 - c], rc.at[0])
            for g in range(6):
                norm(g)
        if t == 13:
            wait_for(dyo.at[1 - c], rc.at[1])
            for g in range(6):
                cotangent(g)

    for t in range(3):
        part = slice(HALF * t, HALF * (t + 1))
        qkv[:, part] = mm3((nh[...], nl[...]), (wh[:, part], wl[:, part]), 1, 0)
    da[...] = mm3((yh[...], yl[...]), (ph[...], plo[...]), 1, 1)
    attention()
    for t in range(3):
        grad_qkv(t)
    for t in range(2):
        grad_proj(t)

    side_send(RORDER[0])
    side_send(RORDER[1])
    for t in range(1, 13):
        if t + 1 < 8:
            side_send(RORDER[t + 1])
        if t == 1:
            project(0)
        if 1 <= t < 9:
            mirror_send(RORDER[t - 1])
        if t == 1:
            project(1)
            send(o_ref.at[1 - c], ob, so_sem.at[2], rb.at[0], mate)
        if 2 <= t < 10:
            y_far(RORDER[t - 2])
        if t in (2, 3, 4):
            grad_input(t - 2)
        if t == 4:
            send(dx_ref.at[1 - c], db, so_sem.at[3], rb.at[1], mate)
            small(0)
        if 3 <= t < 11:
            y_near(RORDER[t - 3])
        if 4 <= t < 12:
            z_step(RORDER[t - 4])
        if t in (6, 8, 10):
            small(t // 2 - 2)
        if t == 2:
            joined(0)
        if 2 <= t <= 5:
            spread(0, 16 * t - 31, min(64, 16 * t - 15))
        if t == 5:
            joined(1)
        if 6 <= t <= 9:
            spread(1, 16 * t - 95, min(64, 16 * t - 79))

    eq[d] = aq[0, 0]
    for there in (side, mate, corner):
        send(eq.at[d], eq.at[d], so_sem.at[15], re.at[0], there)

    @pl.when(holds)
    def _():
        ep[xl] = ap[0, 0]
        for there in (side, mate, corner):
            send(ep.at[xl], ep.at[xl], so_sem.at[16], re.at[1], there)

    wait_for(es.at[pl.ds(0, 3)], re.at[2])
    so[...] = (es[0] + es[2]) + (es[1] + es[3])
    wait_for(eq.at[pl.ds(0, 3)], re.at[0])
    rq[0] = eq[0] + eq[2]
    rq[1] = eq[1] + eq[3]

    @pl.when(holds)
    def _():
        wait_for(ep.at[0], re.at[1])

    @pl.when(jnp.logical_not(holds))
    def _():
        wait_for(ep, re.at[1])

    rp[...] = ep[0] + ep[1]

    wait_for(ob, ro.at[0])
    wait_for(db, ro.at[1])
    wait_for(r1q, so_sem.at[0])
    wait_for(r1p.at[pl.ds(0, 4)], so_sem.at[1])
    wait_for(ob, so_sem.at[2])
    wait_for(db, so_sem.at[3])
    wait_for(smx.at[0], so_sem.at[4])
    wait_for(r2q, so_sem.at[5])
    wait_for(r2p.at[pl.ds(0, 4)], so_sem.at[6])
    wait_for(ob.at[pl.ds(0, 63)], so_sem.at[7])
    wait_for(db.at[pl.ds(0, 63)], so_sem.at[8])
    wait_for(smy.at[pl.ds(0, 3)], so_sem.at[9])
    wait_for(aq.at[:, pl.ds(0, 3)], so_sem.at[10])
    wait_for(ap.at[pl.ds(0, 4), pl.ds(0, 3)], so_sem.at[11])
    wait_for(smz.at[pl.ds(0, 7)], so_sem.at[12])
    wait_for(zq.at[pl.ds(0, 7)], so_sem.at[13])
    wait_for(eq.at[pl.ds(0, 3)], so_sem.at[15])
    wait_for(es.at[pl.ds(0, 3)], so_sem.at[17])

    @pl.when(holds)
    def _():
        wait_for(zp.at[pl.ds(0, 3)], so_sem.at[14])
        wait_for(zp.at[pl.ds(0, 3)], so_sem.at[16])

    @pl.when(jnp.logical_not(holds))
    def _():
        wait_for(zp.at[pl.ds(0, 4)], so_sem.at[14])
    wait_for(wqo.at[pl.ds(0, 7), 0, 0], ss.at[0])
    z_sends = (0, 7, 6, 0, 1, 2)
    for j in z_sends:
        @pl.when(lax.div(lax.rem(z + j, 8), 4) == c)
        def _():
            wait_for(wp_ref, ss.at[1])
    for j, core in ((5, 0), (3, 1)):
        @pl.when(jnp.logical_and(c == core, lax.div(lax.rem(z + j, 8), 4) == c))
        def _():
            wait_for(wp_ref, ss.at[1])
    wait_for(xo.at[0, pl.ds(0, 63)], ss.at[2])
    wait_for(xo.at[0, pl.ds(0, 63)], ss.at[3])
    wait_for(wqo.at[:, pl.ds(0, 3), 0], ss.at[4])
    wait_for(wpo.at[:, pl.ds(0, 3), 0], ss.at[5])
    for sem in (6, 8):
        wait_for(wqo.at[:, :, 0, pl.ds(0, 27)], ss.at[sem])
    for sem in (7, 9):
        wait_for(wpo.at[:, :, 0, pl.ds(0, 9)], ss.at[sem])
    wait_for(xo.at[0], ss.at[10])
    wait_for(xo.at[0], ss.at[11])


def layer(x, dy, wq, wp, vectors):
    dma = pltpu.SemaphoreType.DMA
    anywhere = pl.BlockSpec(memory_space=pl.ANY)
    vmem = pl.BlockSpec(memory_space=pltpu.VMEM)
    act, sml = (64, 9, 2, LANES), (24, LANES)
    q, p = (54, 2, LANES), (18, 4, LANES)
    q2, p2 = (27, 2, LANES), (9, 4, LANES)
    n = HALF

    def buf(*shape):
        return pltpu.VMEM(shape, F32)

    def low(*shape):
        return pltpu.VMEM(shape, BF16)

    return pl.pallas_call(
        layer_kernel,
        out_shape=(
            jax.ShapeDtypeStruct(act, F32),
            jax.ShapeDtypeStruct(act, F32),
            jax.ShapeDtypeStruct((2,) + q, F32),
            jax.ShapeDtypeStruct(p, F32),
            jax.ShapeDtypeStruct(sml, F32),
        ),
        in_specs=[anywhere, anywhere, vmem, vmem, vmem],
        out_specs=(anywhere, anywhere, vmem, vmem, vmem),
        scratch_shapes=[
            buf(108, LANES), buf(72, LANES),
            buf(2304, LANES), buf(2304, LANES), buf(6912, LANES), buf(2304, LANES),
            buf(n, WIDTH), buf(n, LANES), low(n, WIDTH), low(n, WIDTH), low(n, WIDTH), low(n, WIDTH),
            low(WIDTH, 3 * HALF), low(WIDTH, 3 * HALF), low(HALF, WIDTH), low(HALF, WIDTH),
            buf(n, 3 * HALF), buf(n, HALF), low(n, HALF), low(n, HALF), low(n, 3 * HALF), low(n, 3 * HALF),
            buf(2304, LANES), buf(2304, LANES), buf(6912, LANES), buf(2304, LANES), buf(*sml),
            buf(*act), buf(*act),
            buf(8, 4, *q2), buf(8, 4, *p2), buf(8, 4, *q2), buf(8, 4, *p2),
            buf(8, 4, *q), buf(8, 4, *p), buf(8, 2, *q2), buf(8, 2, *p2), buf(8, 2, *q), buf(8, 2, *p),
            buf(9, *q), buf(9, *p), buf(4, *q), buf(2, *p), buf(4, *sml),
            buf(2, *sml), buf(4, *sml), buf(8, *sml),
            dma((12,)), dma((2,)), dma((2, 8)), dma((2, 8, 4)), dma((2, 8, 4)), dma((2, 8, 4)), dma((2,)),
            dma((18,)), dma((2,)), dma((2, 8, 4)), dma((2, 8, 4)), dma((2, 8, 2)), dma((2, 8, 2)), dma((2, 9)),
            dma((2,)), dma((3,)), dma((3,)),
        ],
        compiler_params=pltpu.CompilerParams(
            collective_id=0, has_side_effects=True, vmem_limit_bytes=56 * 1024 * 1024
        ),
    )(x, dy, wq, wp, vectors)


def on_device(
    frames, out_cotangent, layer_norm_gain, layer_norm_bias, qkv_weight, proj_weight, proj_bias
):
    blocks = (64, 9, 2, LANES)
    of, df, rq, rp, so = layer(
        frames.reshape(blocks),
        out_cotangent.reshape(blocks),
        qkv_weight,
        proj_weight,
        jnp.stack([layer_norm_gain, layer_norm_bias]),
    )
    sums = so[:18].reshape(3, WIDTH)
    grad_qkv = jnp.transpose(rq.reshape(2, 12, 3, HALF), (1, 2, 0, 3)).reshape(12, 3 * WIDTH)
    return (
        frames + of.reshape(frames.shape) + proj_bias,
        out_cotangent + df.reshape(frames.shape),
        sums[0],
        sums[1],
        grad_qkv,
        rp.reshape(12, WIDTH),
        sums[2],
    )


def solution(mesh):
    return jax.shard_map(
        on_device,
        mesh=mesh,
        in_specs=(
            P("dp", "seq", None, None),
            P("dp", "seq", None, None),
            P(),
            P(),
            P("seq", None),
            P("seq", None),
            P(),
        ),
        out_specs=(
            P("dp", "seq", None, None),
            P("dp", "seq", None, None),
            P(),
            P(),
            P("seq", None),
            P("seq", None),
            P(),
        ),
        check_vma=False,
    )
```

```python
import jax
import jax.numpy as jnp
from jax import lax
from jax.experimental import pallas as pl
from jax.experimental.pallas import tpu as pltpu
from jax.sharding import PartitionSpec as P

EPSILON = 1e-06
MESH = pl.DeviceIdType.MESH
F32 = jnp.float32
BF16 = jnp.bfloat16
WIDTH = 768
HALF = 384
LANES = 128


def position():
    s = lax.axis_index("seq")
    d = lax.axis_index("dp")
    return s, d, lax.div(s, 8), lax.rem(lax.div(s, 2), 4), lax.rem(s, 2), lax.div(d, 2), lax.rem(d, 2)


def device(s, d):
    return {"seq": s, "dp": d}


def greet(s, d, near):
    barrier = pltpu.get_barrier_semaphore()

    def one(k, carry):
        pl.semaphore_signal(barrier, inc=1, device_id=device(lax.rem(s + k, 64), d), device_id_type=MESH)
        return carry

    lax.fori_loop(1, 64, one, 0)
    for where in near:
        pl.semaphore_signal(barrier, inc=1, device_id=where, device_id_type=MESH)


def others(s, d, xh, xl, c):
    mirror = device(s + 1 - 2 * xh, (1 - xl) * 2 + c)
    side = device(s, (1 - xl) * 2 + c)
    mate = device(s, xl * 2 + 1 - c)
    return mirror, side, mate


def send(src, dst, send_sem, recv_sem, where):
    copy = pltpu.make_async_remote_copy(
        src_ref=src, dst_ref=dst, send_sem=send_sem, recv_sem=recv_sem, device_id=where, device_id_type=MESH
    )
    copy.start()


def wait_for(ref, sem):
    pltpu.make_async_copy(ref, ref, sem).wait()


def split(v):
    high = v.astype(BF16)
    return high, (v - high.astype(F32)).astype(BF16)


def mm(a, b, ca, cb):
    return lax.dot_general(a, b, (((ca,), (cb,)), ((), ())), preferred_element_type=F32)


def mm3(a, b, ca, cb):
    return mm(a[0], b[0], ca, cb) + (mm(a[1], b[0], ca, cb) + mm(a[0], b[1], ca, cb))


def wide(pair):
    return jnp.concatenate(pair, axis=1)


def twice(pair):
    both = wide(pair)
    return jnp.concatenate([both, both], axis=0)


def tall(pair):
    return jnp.concatenate([wide((v, v)) for v in pair], axis=0)


def halves(r):
    return r[:, :LANES] + r[:, LANES:]


def stacked(left, v):
    return jnp.concatenate([jnp.where(left, v, 0.0), jnp.where(left, 0.0, v)], axis=0)


def joined_heads(left, v):
    return jnp.where(left, v[:LANES], v[LANES:])


ORDER = (0, 1, 7, 2, 6, 3, 5, 4)
RORDER = (4, 5, 3, 6, 2, 7, 1, 0)
ROWS = (2, 1, 3, 0)
COLS = [slice(LANES * j, LANES * (j + 1)) for j in range(9)]


def layer_kernel(
    x_raw, dy_raw, wq_raw, wp_raw, gain_ref, bias_ref, pbias_ref, out, dout, rq, rp, so,
    xl2, dyl2, of2, df2, eq2, ep2, wq_own, wp_own, x2, dy2, wq2, wp2,
    xhat, rstd, nh, nl, yh, yl, wh, wl, ph, plo, qkv, da, ah, al, dh, dl, o2, d2, gq2, gp2, sm, pr,
    ob, db, r1q, r1p, r2q, r2p, aq, ap, hq, hp, fq, fp, zq, zp, es, smx, smy, smz,
    ss, rx, rz, ry, rm, rs, rc, so_sem, rb, r1s, r2s, rh, rf, rzz, ro, ra, re,
):
    s, d, z, y, xh, xl, c = position()
    mirror, side, mate = others(s, d, xh, xl, c)
    corner = device(s, (1 - xl) * 2 + 1 - c)
    greet(s, d, (mirror, side, mate, corner))
    holds = lax.div(z, 4) == c
    for t in range(3):
        for n in range(3):
            at = pl.multiple_of(WIDTH * t + HALF * c + LANES * n, LANES)
            wq_own[pl.ds(3 * t + n, 12, stride=9), :] = wq_raw[:, pl.ds(at, LANES)]
    for n in range(6):
        wp_own[pl.ds(n, 12, stride=6), :] = wp_raw[:, COLS[n]]
    sm[...] = jnp.zeros((24, LANES), F32)
    x_ref, dy_ref = xl2.reshape(64, 9, 2, LANES), dyl2.reshape(64, 9, 2, LANES)
    of, df = of2.reshape(64, 9, 2, LANES), df2.reshape(64, 9, 2, LANES)
    eq, ep = eq2.reshape(4, 54, 2, LANES), ep2.reshape(2, 18, 4, LANES)
    wq_ref, wp_ref = wq_own.reshape(54, 2, LANES), wp_own.reshape(18, 4, LANES)
    xo, dyo = x2.reshape(2, 64, 9, 2, LANES), dy2.reshape(2, 64, 9, 2, LANES)
    o_ref, dx_ref = o2.reshape(2, 64, 9, 2, LANES), d2.reshape(2, 64, 9, 2, LANES)
    wqo, wpo = wq2.reshape(8, 4, 2, 54, 2, LANES), wp2.reshape(4, 4, 2, 18, 4, LANES)
    gq_ref, gp_ref = gq2.reshape(8, 4, 2, 54, 2, LANES), gp2.reshape(4, 4, 2, 18, 4, LANES)
    pl.semaphore_wait(pltpu.get_barrier_semaphore(), 67)

    def zdev(k):
        return device((lax.rem(z + k + 8, 8) * 4 + y) * 2 + xh, d)

    def ydev(k):
        return device((z * 4 + lax.rem(y + k, 4)) * 2 + xh, d)

    def both(part, j, q_job, p_job):
        at = lax.rem(z + j, 8)
        if part == "q":
            q_job(at)
        else:
            @pl.when(lax.div(at, 4) == c)
            def _():
                p_job(lax.rem(at, 4))

    def along_z(part, j, to, there, src_q=None, src_p=None):
        both(
            part,
            j,
            lambda at: send(wqo.at[at, y, xh] if src_q is None else src_q, wqo.at[at, y, xh], ss.at[0], rz.at[0, to], there),
            lambda at: send(wpo.at[at, y, xh] if src_p is None else src_p, wpo.at[at, y, xh], ss.at[1], rz.at[1, to], there),
        )

    def z_stage(part, j):
        if j == 0:
            along_z(part, 0, 7, zdev(1), wq_ref, wp_ref)
            along_z(part, 0, 1, zdev(-1), wq_ref, wp_ref)
            both(
                part,
                0,
                lambda at: pltpu.make_async_copy(wq_ref, wqo.at[at, y, xh], rz.at[0, 0]).start(),
                lambda at: pltpu.make_async_copy(wp_ref, wpo.at[at, y, xh], rz.at[1, 0]).start(),
            )
        both(
            part,
            j,
            lambda at: wait_for(wqo.at[at, y, xh], rz.at[0, j]),
            lambda at: wait_for(wpo.at[at, y, xh], rz.at[1, j]),
        )
        if j in (7, 6):
            along_z(part, j, j - 1, zdev(1))
        if j in (1, 2):
            along_z(part, j, j + 1, zdev(-1))
        if j == 5:
            @pl.when(c == 0)
            def _():
                along_z(part, 5, 4, zdev(1))
        if j == 3:
            @pl.when(c == 1)
            def _():
                along_z(part, 3, 4, zdev(-1))

    def y_send(part, j):
        for k in (1, 3):
            both(
                part,
                j,
                lambda at: send(wqo.at[at, y, xh], wqo.at[at, y, xh], ss.at[4], ry.at[0, j, k], ydev(k)),
                lambda at: send(wpo.at[at, y, xh], wpo.at[at, y, xh], ss.at[5], ry.at[1, j, k], ydev(k)),
            )

    def across(part, j, k):
        row = lax.rem(y + 4 - k, 4)
        hq, hp = pl.ds(27 * (1 - xl), 27), pl.ds(9 * (1 - xl), 9)

        def q(at):
            ref = wqo.at[at, row, xh, hq]
            send(ref, ref, ss.at[6], rm.at[0, j, row], mirror)

        def p(at):
            ref = wpo.at[at, row, xh, hp]
            send(ref, ref, ss.at[7], rm.at[1, j, row], mirror)

        both(part, j, q, p)

    def y_wait(part, j, k):
        row = lax.rem(y + 4 - k, 4)
        both(
            part,
            j,
            lambda at: wait_for(wqo.at[at, row, xh], ry.at[0, j, k]),
            lambda at: wait_for(wpo.at[at, row, xh], ry.at[1, j, k]),
        )

    def y_pass(part, j, k):
        h = 0 if k == 1 else 1
        row = lax.rem(y + 4 - k, 4)

        def q(at):
            ref = wqo.at[at, row, xh, pl.ds(27 * h, 27)]
            send(ref, ref, ss.at[4], ry.at[0, j, 2], ydev(k))

        def p(at):
            ref = wpo.at[at, row, xh, pl.ds(9 * h, 9)]
            send(ref, ref, ss.at[5], ry.at[1, j, 2], ydev(k))

        both(part, j, q, p)

    def forward(part, j, k):
        row = lax.rem(y + 4 - k, 4)
        hq, hp = pl.ds(27 * xl, 27), pl.ds(9 * xl, 9)

        def q(at):
            ref = wqo.at[at, row, 1 - xh, hq]
            wait_for(ref, rm.at[0, j, row])
            send(ref, ref, ss.at[8], rs.at[0, j, row], side)

        def p(at):
            ref = wpo.at[at, row, 1 - xh, hp]
            wait_for(ref, rm.at[1, j, row])
            send(ref, ref, ss.at[9], rs.at[1, j, row], side)

        both(part, j, q, p)

    def lay_out(n):
        raw, line, src, dst = ((x_raw, xl2, x_ref, xo), (dy_raw, dyl2, dy_ref, dyo))[n]
        for i in range(6):
            line[pl.ds(i, 192, stride=6), :] = raw[:, COLS[i]]
        pltpu.make_async_copy(src.at[s], dst.at[c, s], rx.at[n]).start()

    def spread_in(n, first, last):
        src, dst = ((x_ref, xo), (dy_ref, dyo))[n]

        def one(k, carry):
            t = lax.rem(s + k, 64)
            send(src.at[t], dst.at[c, s], ss.at[2 + n], rx.at[n], device(t, d))
            return carry

        lax.fori_loop(first, last, one, 0)

    gain = gain_ref[...].reshape(1, WIDTH)
    bias = bias_ref[...].reshape(1, WIDTH)
    pbias = pbias_ref[...].reshape(1, WIDTH)

    def weights(part, j):
        at = lax.rem(z + j, 8)
        for k in range(4):
            row = lax.rem(y + 4 - k, 4)
            both(
                part,
                j,
                lambda at: wait_for(wqo.at[at, row, 1 - xh, pl.ds(27 * (1 - xl), 27)], rs.at[0, j, row]),
                lambda at: wait_for(wpo.at[at, row, 1 - xh, pl.ds(9 * (1 - xl), 9)], rs.at[1, j, row]),
            )

        def q(at):
            rows = pl.ds(pl.multiple_of(at * 96, 96), 96)
            for n in range(9):
                wh[rows, COLS[n]], wl[rows, COLS[n]] = split(wq2[pl.ds(at * 864 + n, 96, stride=9), :])

        def p(at):
            rows = pl.ds(pl.multiple_of(at * 96, 96), 96)
            for n in range(6):
                ph[rows, COLS[n]], plo[rows, COLS[n]] = split(wp2[pl.ds(at * 576 + n, 96, stride=6), :])

        both(part, j, q, p)

    def tokens(ref, g):
        base = (g // 3) * 1152 + (g % 3) * 6
        return jnp.concatenate([ref[pl.ds(base + n, 64, stride=18), :] for n in range(6)], axis=1)

    def norm(g):
        rows = slice(64 * g, 64 * (g + 1))
        v = tokens(x2, g)
        centred = v - jnp.mean(v, axis=1, keepdims=True)
        r = lax.rsqrt(jnp.mean(centred * centred, axis=1, keepdims=True) + EPSILON)
        hat = centred * r
        xhat[rows, :] = hat
        rstd[rows, :] = jnp.broadcast_to(r, (64, LANES))
        nh[rows, :], nl[rows, :] = split(hat * gain + bias)

    def cotangent(g):
        rows = slice(64 * g, 64 * (g + 1))
        v = tokens(dy2, g)
        yh[rows, :], yl[rows, :] = split(v)
        add_small(12, jnp.sum(v, axis=0, keepdims=True) * 0.5)

    def add_small(first, v):
        for n in range(6):
            at = slice(first + n, first + n + 1)
            sm[at, :] = sm[at, :] + v[:, COLS[n]]

    def query_key_value(t):
        cols = slice(HALF * t, HALF * (t + 1))
        qkv[:, cols] = mm3((nh[...], nl[...]), (wh[:, cols], wl[:, cols]), 1, 0)

    def d_attended():
        da[...] = mm3((yh[...], yl[...]), (ph[...], plo[...]), 1, 1)

    left = lax.broadcasted_iota(jnp.int32, (LANES, LANES), 1) < 64
    scale = 0.125

    def operands(rows, h):
        q = wide(split(stacked(left, qkv[rows, COLS[h]] * scale)))
        return q, split(qkv[rows, COLS[3 + h]]), split(qkv[rows, COLS[6 + h]])

    def forward_attention(i):
        rows = slice(LANES * i, LANES * (i + 1))
        first = lax.broadcasted_iota(jnp.int32, (2 * LANES, LANES), 0) % LANES < 64
        same = first == (lax.broadcasted_iota(jnp.int32, (2 * LANES, LANES), 1) < 64)
        for h in range(3):
            q, k, v = operands(rows, h)
            scores = jnp.where(same, halves(mm(q, tall(k), 1, 1)), -1e30)
            e = jnp.exp(scores - jnp.max(scores, axis=1, keepdims=True))
            probs = e / jnp.sum(e, axis=1, keepdims=True)
            pr[3 * i + h] = probs
            attended = joined_heads(left, halves(mm(wide(split(probs)), twice(v), 1, 0)))
            ah[rows, COLS[h]], al[rows, COLS[h]] = split(attended)

    def backward_attention(i):
        rows = slice(LANES * i, LANES * (i + 1))

        def over_rows(a, b):
            r = halves(mm(a, b, 0, 0))
            return r[:LANES] + r[LANES:]

        for h in range(3):
            q, k, v = operands(rows, h)
            a = wide(split(stacked(left, da[rows, COLS[h]])))
            probs = pr[3 * i + h]
            dh[rows, COLS[6 + h]], dl[rows, COLS[6 + h]] = split(over_rows(wide(split(probs)), a))
            t = halves(mm(a, tall(v), 1, 1)) * probs
            ds = wide(split(t - probs * jnp.sum(t, axis=1, keepdims=True)))
            dq = joined_heads(left, halves(mm(ds, twice(k), 1, 0))) * scale
            dh[rows, COLS[h]], dl[rows, COLS[h]] = split(dq)
            dh[rows, COLS[3 + h]], dl[rows, COLS[3 + h]] = split(over_rows(ds, q))

    def project(t):
        part = slice(HALF * t, HALF * (t + 1))
        o = mm3((ah[...], al[...]), (ph[:, part], plo[:, part]), 1, 0)
        for g in range(6):
            for n in range(3):
                at = pl.ds((g // 3) * 1152 + (g % 3) * 6 + 3 * t + n, 64, stride=18)
                own = x2[at, :] + pbias[:, COLS[3 * t + n]]
                o2[at, :] = o[64 * g : 64 * (g + 1), COLS[n]] + jnp.where(c == g // 3, own, 0.0)

    def grad_proj(t):
        part = slice(HALF * t, HALF * (t + 1))
        w = mm3((ah[...], al[...]), (yh[:, part], yl[:, part]), 0, 0)
        for n in range(3):
            gp2[pl.ds(3 * t + n, HALF, stride=6), :] = w[:, COLS[n]]

    def grad_qkv(t):
        part = slice(HALF * t, HALF * (t + 1))
        w = mm3((nh[...], nl[...]), (dh[:, part], dl[:, part]), 0, 0)
        for n in range(3):
            gq2[pl.ds(3 * t + n, WIDTH, stride=9), :] = w[:, COLS[n]]

    def grad_input(i):
        dn = mm3((dh[128 * i : 128 * (i + 1), :], dl[128 * i : 128 * (i + 1), :]), (wh[...], wl[...]), 1, 1)
        for half in range(2):
            g = 2 * i + half
            rows = slice(64 * g, 64 * (g + 1))
            n = dn[64 * half : 64 * (half + 1)]
            hat = xhat[rows, :]
            add_small(0, jnp.sum(n * hat, axis=0, keepdims=True))
            add_small(6, jnp.sum(n, axis=0, keepdims=True))
            n = n * gain
            m1 = jnp.mean(n, axis=1, keepdims=True)
            m2 = jnp.mean(n * hat, axis=1, keepdims=True)
            dx = rstd[rows, 0:1] * (n - m1 - hat * m2)
            for j in range(6):
                at = pl.ds((g // 3) * 1152 + (g % 3) * 6 + j, 64, stride=18)
                d2[at, :] = dx[:, COLS[j]] + jnp.where(c == g // 3, dy2[at, :], 0.0)

    oxh = 1 - xh
    mine_q, mine_p = pl.ds(27 * xl, 27), pl.ds(9 * xl, 9)
    yours_q, yours_p = pl.ds(27 * (1 - xl), 27), pl.ds(9 * (1 - xl), 9)

    def row(k):
        return lax.rem(y + k, 4)

    def side_send(part, j):
        for k in ROWS:
            both(
                part,
                j,
                lambda at: send(gq_ref.at[at, row(k), oxh, yours_q], r1q.at[j, k], so_sem.at[0], r1s.at[0, j, k], side),
                lambda at: send(gp_ref.at[at, row(k), oxh, yours_p], r1p.at[j, k], so_sem.at[1], r1s.at[1, j, k], side),
            )

    def mirror_send(part, j):
        for k in ROWS:
            def q(at):
                wait_for(r1q.at[j, k], r1s.at[0, j, k])
                r1q[j, k] = r1q[j, k] + gq_ref[at, row(k), oxh, mine_q]
                send(r1q.at[j, k], r2q.at[j, k], so_sem.at[5], r2s.at[0, j, k], mirror)

            def p(at):
                wait_for(r1p.at[j, k], r1s.at[1, j, k])
                r1p[j, k] = r1p[j, k] + gp_ref[at, row(k), oxh, mine_p]
                send(r1p.at[j, k], r2p.at[j, k], so_sem.at[6], r2s.at[1, j, k], mirror)

            both(part, j, q, p)

    def gather(part, j, k):
        def q(at):
            wait_for(r2q.at[j, k], r2s.at[0, j, k])
            aq[j, k, mine_q] = gq_ref[at, row(k), xh, mine_q]
            aq[j, k, yours_q] = gq_ref[at, row(k), xh, yours_q] + r2q[j, k]

        def p(at):
            wait_for(r2p.at[j, k], r2s.at[1, j, k])
            ap[j, k, mine_p] = gp_ref[at, row(k), xh, mine_p]
            ap[j, k, yours_p] = gp_ref[at, row(k), xh, yours_p] + r2p[j, k]

        both(part, j, q, p)

    def y_far(part, j):
        gather(part, j, 2)
        for n, k in ((0, 1), (1, 3)):
            both(
                part,
                j,
                lambda at: send(aq.at[j, 2, pl.ds(27 * n, 27)], hq.at[j, n], so_sem.at[10], rh.at[0, j, n], ydev(k)),
                lambda at: send(ap.at[j, 2, pl.ds(9 * n, 9)], hp.at[j, n], so_sem.at[11], rh.at[1, j, n], ydev(k)),
            )

    def y_near(part, j):
        for n, k in ((0, 1), (1, 3)):
            gather(part, j, k)

            def q(at):
                wait_for(hq.at[j, n], rh.at[0, j, n])
                piece = pl.ds(27 * n, 27)
                aq[j, k, piece] = aq[j, k, piece] + hq[j, n]
                send(aq.at[j, k], fq.at[j, n], so_sem.at[10], rf.at[0, j, n], ydev(k))

            def p(at):
                wait_for(hp.at[j, n], rh.at[1, j, n])
                piece = pl.ds(9 * n, 9)
                ap[j, k, piece] = ap[j, k, piece] + hp[j, n]
                send(ap.at[j, k], fp.at[j, n], so_sem.at[11], rf.at[1, j, n], ydev(k))

            both(part, j, q, p)

    def z_step(part, j):
        gather(part, j, 0)

        def q(at):
            wait_for(fq.at[j, 0], rf.at[0, j, 0])
            wait_for(fq.at[j, 1], rf.at[0, j, 1])
            aq[j, 0] = aq[j, 0] + (fq[j, 0] + fq[j, 1])

        def p(at):
            wait_for(fp.at[j, 0], rf.at[1, j, 0])
            wait_for(fp.at[j, 1], rf.at[1, j, 1])
            ap[j, 0] = ap[j, 0] + (fp[j, 0] + fp[j, 1])

        both(part, j, q, p)

        def come(slot):
            def q(at):
                wait_for(zq.at[slot], rzz.at[0, slot])
                aq[j, 0] = aq[j, 0] + zq[slot]

            def p(at):
                wait_for(zp.at[slot], rzz.at[1, slot])
                ap[j, 0] = ap[j, 0] + zp[slot]

            both(part, j, q, p)

        def go(slot, k):
            both(
                part,
                j,
                lambda at: send(aq.at[j, 0], zq.at[slot], so_sem.at[13], rzz.at[0, slot], zdev(k)),
                lambda at: send(ap.at[j, 0], zp.at[slot], so_sem.at[14], rzz.at[1, slot], zdev(k)),
            )

        if j == 4:
            @pl.when(c == 0)
            def _():
                go(3, 1)

            @pl.when(c == 1)
            def _():
                go(5, -1)
        elif j == 0:
            come(0)
            come(8)
        else:
            if j in (3, 5):
                @pl.when(c == (0 if j == 3 else 1))
                def _():
                    come(j)
            else:
                come(j)
            if j < 4:
                go(j - 1, 1)
            else:
                go(j + 1, -1)

    def joined(n):
        own, buf, out = ((o_ref, ob, of), (dx_ref, db, df))[n]
        wait_for(buf, rb.at[n])

        def add(i, carry):
            at = pl.ds(8 * i, 8)
            buf[at] = buf[at] + own[c, at]
            return carry

        lax.fori_loop(0, 8, add, 0)
        pltpu.make_async_copy(buf.at[s], out.at[s], ro.at[n]).start()

    def spread(n, first, last):
        buf, out = ((ob, of), (db, df))[n]

        def one(k, carry):
            t = lax.rem(s + k, 64)
            send(buf.at[t], out.at[s], so_sem.at[7 + n], ro.at[n], device(t, d))
            return carry

        lax.fori_loop(first, last, one, 0)

    def small(step):
        if step == 0:
            smx[0] = sm[...]
            send(smx.at[0], smx.at[1], so_sem.at[4], ra.at[0], mirror)
        if step == 1:
            wait_for(smx.at[1], ra.at[0])
            smy[y] = smx[0] + smx[1]
            for k in range(1, 4):
                send(smy.at[y], smy.at[y], so_sem.at[9], ra.at[1], ydev(k))
        if step == 2:
            wait_for(smy.at[pl.ds(0, 3)], ra.at[1])
            smz[z] = (smy[0] + smy[1]) + (smy[2] + smy[3])
            for k in range(1, 8):
                send(smz.at[z], smz.at[z], so_sem.at[12], ra.at[2], zdev(k))
        if step == 3:
            wait_for(smz.at[pl.ds(0, 7)], ra.at[2])
            es[d] = ((smz[0] + smz[1]) + (smz[2] + smz[3])) + ((smz[4] + smz[5]) + (smz[6] + smz[7]))
            for there in (side, mate, corner):
                send(es.at[d], es.at[d], so_sem.at[17], re.at[2], there)

    def step_in(part, t):
        if 0 <= t < 8:
            z_stage(part, ORDER[t])
            y_send(part, ORDER[t])
            across(part, ORDER[t], 0)
        if 1 <= t < 9:
            j = ORDER[t - 1]
            for k in (1, 3):
                y_wait(part, j, k)
                y_pass(part, j, k)
                across(part, j, k)
        if 2 <= t < 10:
            j = ORDER[t - 2]
            y_wait(part, j, 2)
            across(part, j, 2)
            forward(part, j, 0)
        if 3 <= t < 11:
            j = ORDER[t - 3]
            for k in (1, 3, 2):
                forward(part, j, k)
        if 6 <= t < 14:
            weights(part, ORDER[t - 6])

    def step_out(part, t):
        if 0 <= t + 1 < 8:
            side_send(part, RORDER[t + 1])
        if 1 <= t < 9:
            mirror_send(part, RORDER[t - 1])
        if 2 <= t < 10:
            y_far(part, RORDER[t - 2])
        if 3 <= t < 11:
            y_near(part, RORDER[t - 3])
        if 4 <= t < 12:
            z_step(part, RORDER[t - 4])

    for t in range(14):
        step_in("q", t)
        step_in("p", t - 0)
        if t == 0:
            lay_out(0)
        if t == 4:
            lay_out(1)
        if t == 1:
            spread_in(0, 1, 16)
        if t == 2:
            spread_in(0, 16, 32)
        if t == 3:
            spread_in(0, 32, 48)
        if t == 4:
            spread_in(0, 48, 64)
        if t == 5:
            spread_in(1, 1, 16)
        if t == 6:
            spread_in(1, 16, 32)
        if t == 7:
            spread_in(1, 32, 48)
        if t == 8:
            spread_in(1, 48, 64)
        if t == 10:
            wait_for(xo.at[c], rx.at[0])
            send(xo.at[c], xo.at[c], ss.at[10], rc.at[0], mate)
        if t == 11:
            wait_for(dyo.at[c], rx.at[1])
            send(dyo.at[c], dyo.at[c], ss.at[11], rc.at[1], mate)
        if t == 12:
            wait_for(xo.at[1 - c], rc.at[0])
            for g in range(6):
                norm(g)
        if t == 13:
            wait_for(dyo.at[1 - c], rc.at[1])
            for g in range(6):
                cotangent(g)
        if 13 <= t < 13 + 0:
            query_key_value(t - 13)
    for t in range(0, 3):
        query_key_value(t)
    for i in range(3):
        forward_attention(i)
    project(0)
    project(1)
    send(o_ref.at[1 - c], ob, so_sem.at[2], rb.at[0], mate)
    grad_proj(0)
    grad_proj(1)
    d_attended()
    for t in range(3):
        backward_attention(t)
    for n in range(3):
        grad_qkv(n)
    for t in range(-1, 12):
        step_out("p", t)
        step_out("q", t - 0)
        if t == 0:
            joined(0)
        if t == 1:
            spread(0, 1, 16)
        if t == 1:
            spread(0, 16, 32)
        if t == 1:
            grad_input(0)
        if t == 2:
            spread(0, 32, 48)
        if t == 2:
            spread(0, 48, 64)
        if t == 2:
            grad_input(1)
        if t == 3:
            grad_input(2)
        if t == 3:
            send(dx_ref.at[1 - c], db, so_sem.at[3], rb.at[1], mate)
        if t == 3:
            small(0)
        if t == 4:
            joined(1)
        if t == 4:
            spread(1, 1, 22)
        if t == 5:
            spread(1, 22, 43)
        if t == 5:
            small(1)
        if t == 6:
            spread(1, 43, 64)
        if t == 7:
            small(2)
        if t == 9:
            small(3)

    eq[d] = aq[0, 0]
    for there in (side, mate, corner):
        send(eq.at[d], eq.at[d], so_sem.at[15], re.at[0], there)

    @pl.when(holds)
    def _():
        ep[xl] = ap[0, 0]
        for there in (side, mate, corner):
            send(ep.at[xl], ep.at[xl], so_sem.at[16], re.at[1], there)

    wait_for(es.at[pl.ds(0, 3)], re.at[2])
    so[...] = (es[0] + es[2]) + (es[1] + es[3])
    wait_for(eq.at[pl.ds(0, 3)], re.at[0])
    for h in range(2):
        for n in range(9):
            at = WIDTH * (n // 3) + HALF * h + LANES * (n % 3)
            rq[:, at : at + LANES] = (
                eq2[pl.ds(108 * h + n, 12, stride=9), :] + eq2[pl.ds(108 * (h + 2) + n, 12, stride=9), :]
            )

    @pl.when(holds)
    def _():
        wait_for(ep.at[0], re.at[1])

    @pl.when(jnp.logical_not(holds))
    def _():
        wait_for(ep, re.at[1])

    for n in range(6):
        rp[:, COLS[n]] = ep2[pl.ds(n, 12, stride=6), :] + ep2[pl.ds(72 + n, 12, stride=6), :]

    wait_for(ob, ro.at[0])
    wait_for(db, ro.at[1])
    for i in range(6):
        out[:, COLS[i]] = of2[pl.ds(i, 192, stride=6), :]
        dout[:, COLS[i]] = df2[pl.ds(i, 192, stride=6), :]
    wait_for(r1q, so_sem.at[0])
    wait_for(r1p.at[pl.ds(0, 4)], so_sem.at[1])
    wait_for(ob, so_sem.at[2])
    wait_for(db, so_sem.at[3])
    wait_for(smx.at[0], so_sem.at[4])
    wait_for(r2q, so_sem.at[5])
    wait_for(r2p.at[pl.ds(0, 4)], so_sem.at[6])
    wait_for(ob.at[pl.ds(0, 63)], so_sem.at[7])
    wait_for(db.at[pl.ds(0, 63)], so_sem.at[8])
    wait_for(smy.at[pl.ds(0, 3)], so_sem.at[9])
    wait_for(aq.at[:, pl.ds(0, 3)], so_sem.at[10])
    wait_for(ap.at[pl.ds(0, 4), pl.ds(0, 3)], so_sem.at[11])
    wait_for(smz.at[pl.ds(0, 7)], so_sem.at[12])
    wait_for(zq.at[pl.ds(0, 7)], so_sem.at[13])
    wait_for(eq.at[pl.ds(0, 3)], so_sem.at[15])
    wait_for(es.at[pl.ds(0, 3)], so_sem.at[17])

    @pl.when(holds)
    def _():
        wait_for(zp.at[pl.ds(0, 3)], so_sem.at[14])
        wait_for(zp.at[pl.ds(0, 3)], so_sem.at[16])

    @pl.when(jnp.logical_not(holds))
    def _():
        wait_for(zp.at[pl.ds(0, 4)], so_sem.at[14])
    wait_for(wqo.at[pl.ds(0, 7), 0, 0], ss.at[0])
    z_sends = (0, 7, 6, 0, 1, 2)
    for j in z_sends:
        @pl.when(lax.div(lax.rem(z + j, 8), 4) == c)
        def _():
            wait_for(wp_ref, ss.at[1])
    for j, core in ((5, 0), (3, 1)):
        @pl.when(jnp.logical_and(c == core, lax.div(lax.rem(z + j, 8), 4) == c))
        def _():
            wait_for(wp_ref, ss.at[1])
    wait_for(xo.at[0, pl.ds(0, 63)], ss.at[2])
    wait_for(xo.at[0, pl.ds(0, 63)], ss.at[3])
    wait_for(wqo.at[:, pl.ds(0, 3), 0], ss.at[4])
    wait_for(wpo.at[:, pl.ds(0, 3), 0], ss.at[5])
    for sem in (6, 8):
        wait_for(wqo.at[:, :, 0, pl.ds(0, 27)], ss.at[sem])
    for sem in (7, 9):
        wait_for(wpo.at[:, :, 0, pl.ds(0, 9)], ss.at[sem])
    wait_for(xo.at[0], ss.at[10])
    wait_for(xo.at[0], ss.at[11])


def layer(x, dy, wq, wp, gain, bias, pbias):
    dma = pltpu.SemaphoreType.DMA
    vmem = pl.BlockSpec(memory_space=pltpu.VMEM)
    act, sml = (64, 9, 2, LANES), (24, LANES)
    q, p = (54, 2, LANES), (18, 4, LANES)
    q2, p2 = (27, 2, LANES), (9, 4, LANES)
    n = HALF

    def buf(*shape):
        return pltpu.VMEM(shape, F32)

    def low(*shape):
        return pltpu.VMEM(shape, BF16)

    return pl.pallas_call(
        layer_kernel,
        out_shape=(
            jax.ShapeDtypeStruct((192, WIDTH), F32),
            jax.ShapeDtypeStruct((192, WIDTH), F32),
            jax.ShapeDtypeStruct((12, 3 * WIDTH), F32),
            jax.ShapeDtypeStruct((12, WIDTH), F32),
            jax.ShapeDtypeStruct(sml, F32),
        ),
        in_specs=[vmem] * 7,
        out_specs=(vmem,) * 5,
        scratch_shapes=[
            buf(1152, LANES), buf(1152, LANES), buf(1152, LANES), buf(1152, LANES), buf(432, LANES), buf(144, LANES),
            buf(108, LANES), buf(72, LANES),
            buf(2304, LANES), buf(2304, LANES), buf(6912, LANES), buf(2304, LANES),
            buf(n, WIDTH), buf(n, LANES), low(n, WIDTH), low(n, WIDTH), low(n, WIDTH), low(n, WIDTH),
            low(WIDTH, 3 * HALF), low(WIDTH, 3 * HALF), low(HALF, WIDTH), low(HALF, WIDTH),
            buf(n, 3 * HALF), buf(n, HALF), low(n, HALF), low(n, HALF), low(n, 3 * HALF), low(n, 3 * HALF),
            buf(2304, LANES), buf(2304, LANES), buf(6912, LANES), buf(2304, LANES), buf(*sml), buf(9, 2 * LANES, LANES),
            buf(*act), buf(*act),
            buf(8, 4, *q2), buf(8, 4, *p2), buf(8, 4, *q2), buf(8, 4, *p2),
            buf(8, 4, *q), buf(8, 4, *p), buf(8, 2, *q2), buf(8, 2, *p2), buf(8, 2, *q), buf(8, 2, *p),
            buf(9, *q), buf(9, *p), buf(4, *sml),
            buf(2, *sml), buf(4, *sml), buf(8, *sml),
            dma((12,)), dma((2,)), dma((2, 8)), dma((2, 8, 4)), dma((2, 8, 4)), dma((2, 8, 4)), dma((2,)),
            dma((18,)), dma((2,)), dma((2, 8, 4)), dma((2, 8, 4)), dma((2, 8, 2)), dma((2, 8, 2)), dma((2, 9)),
            dma((2,)), dma((3,)), dma((3,)),
        ],
        compiler_params=pltpu.CompilerParams(
            collective_id=0, has_side_effects=True, vmem_limit_bytes=56 * 1024 * 1024
        ),
    )(x, dy, wq, wp, gain, bias, pbias)


def on_device(
    frames, out_cotangent, layer_norm_gain, layer_norm_bias, qkv_weight, proj_weight, proj_bias
):
    out, dout, rq, rp, so = layer(
        frames.reshape(192, WIDTH),
        out_cotangent.reshape(192, WIDTH),
        qkv_weight,
        proj_weight,
        layer_norm_gain,
        layer_norm_bias,
        proj_bias,
    )
    sums = so[:18].reshape(3, WIDTH)
    return (
        out.reshape(frames.shape),
        dout.reshape(frames.shape),
        sums[0],
        sums[1],
        rq,
        rp,
        sums[2],
    )


def solution(mesh):
    return jax.shard_map(
        on_device,
        mesh=mesh,
        in_specs=(
            P("dp", "seq", None, None),
            P("dp", "seq", None, None),
            P(),
            P(),
            P("seq", None),
            P("seq", None),
            P(),
        ),
        out_specs=(
            P("dp", "seq", None, None),
            P("dp", "seq", None, None),
            P(),
            P(),
            P("seq", None),
            P("seq", None),
            P(),
        ),
        check_vma=False,
    )
```

```python
import jax
import jax.numpy as jnp
from jax import lax
from jax.experimental import pallas as pl
from jax.experimental.pallas import tpu as pltpu
from jax.sharding import PartitionSpec as P

EPSILON = 1e-06
MESH = pl.DeviceIdType.MESH
F32 = jnp.float32
BF16 = jnp.bfloat16
WIDTH = 768
HALF = 384
LANES = 128


def position():
    s = lax.axis_index("seq")
    d = lax.axis_index("dp")
    return s, d, lax.div(s, 8), lax.rem(lax.div(s, 2), 4), lax.rem(s, 2), lax.div(d, 2), lax.rem(d, 2)


def device(s, d):
    return {"seq": s, "dp": d}


def greet(s, d, near):
    barrier = pltpu.get_barrier_semaphore()

    def one(k, carry):
        pl.semaphore_signal(barrier, inc=1, device_id=device(lax.rem(s + k, 64), d), device_id_type=MESH)
        return carry

    lax.fori_loop(1, 64, one, 0)
    for where in near:
        pl.semaphore_signal(barrier, inc=1, device_id=where, device_id_type=MESH)


def others(s, d, xh, xl, c):
    mirror = device(s + 1 - 2 * xh, (1 - xl) * 2 + c)
    side = device(s, (1 - xl) * 2 + c)
    mate = device(s, xl * 2 + 1 - c)
    return mirror, side, mate


def send(src, dst, send_sem, recv_sem, where):
    copy = pltpu.make_async_remote_copy(
        src_ref=src, dst_ref=dst, send_sem=send_sem, recv_sem=recv_sem, device_id=where, device_id_type=MESH
    )
    copy.start()


def wait_for(ref, sem):
    pltpu.make_async_copy(ref, ref, sem).wait()


def split(v):
    high = v.astype(BF16)
    return high, (v - high.astype(F32)).astype(BF16)


def mm(a, b, ca, cb):
    return lax.dot_general(a, b, (((ca,), (cb,)), ((), ())), preferred_element_type=F32)


def mm3(a, b, ca, cb):
    return mm(a[0], b[0], ca, cb) + (mm(a[1], b[0], ca, cb) + mm(a[0], b[1], ca, cb))


def wide(pair):
    return jnp.concatenate(pair, axis=1)


def twice(pair):
    both = wide(pair)
    return jnp.concatenate([both, both], axis=0)


def tall(pair):
    return jnp.concatenate([wide((v, v)) for v in pair], axis=0)


def halves(r):
    return r[:, :LANES] + r[:, LANES:]


def stacked(left, v):
    return jnp.concatenate([jnp.where(left, v, 0.0), jnp.where(left, 0.0, v)], axis=0)


def joined_heads(left, v):
    return jnp.where(left, v[:LANES], v[LANES:])


ORDER = (0, 1, 7, 2, 6, 3, 5, 4)
RORDER = (4, 5, 3, 6, 2, 7, 1, 0)
ROWS = (2, 1, 3, 0)
COLS = [slice(LANES * j, LANES * (j + 1)) for j in range(9)]


def layer_kernel(
    x_hbm, dy_hbm, wq_raw, wp_raw, gain_ref, bias_ref, pbias_ref, out, dout, rq, rp, so,
    x_raw, dy_raw, fetched, xl2, dyl2, of2, df2, eq2, ep2, wq_own, wp_own, x2, dy2, wq2, wp2,
    xhat, rstd, nh, nl, yh, yl, wh, wl, ph, plo, qkv, da, ah, al, dh, dl, o2, d2, gq2, gp2, sm, pr,
    ob, db, r1q, r1p, r2q, r2p, aq, ap, hq, hp, fq, fp, zq, zp, es, smx, smy, smz,
    ss, rx, rz, ry, rm, rs, rc, so_sem, rb, r1s, r2s, rh, rf, rzz, ro, ra, re,
):
    s, d, z, y, xh, xl, c = position()
    mirror, side, mate = others(s, d, xh, xl, c)
    corner = device(s, (1 - xl) * 2 + 1 - c)
    greet(s, d, (mirror, side, mate, corner))
    x_fetch = pltpu.make_async_copy(x_hbm, x_raw, fetched.at[0])
    dy_fetch = pltpu.make_async_copy(dy_hbm, dy_raw, fetched.at[1])
    x_fetch.start()
    dy_fetch.start()
    holds = lax.div(z, 4) == c
    for t in range(3):
        for n in range(3):
            at = pl.multiple_of(WIDTH * t + HALF * c + LANES * n, LANES)
            wq_own[pl.ds(3 * t + n, 12, stride=9), :] = wq_raw[:, pl.ds(at, LANES)]
    for n in range(6):
        wp_own[pl.ds(n, 12, stride=6), :] = wp_raw[:, COLS[n]]
    sm[...] = jnp.zeros((24, LANES), F32)
    x_ref, dy_ref = xl2.reshape(64, 9, 2, LANES), dyl2.reshape(64, 9, 2, LANES)
    of, df = of2.reshape(64, 9, 2, LANES), df2.reshape(64, 9, 2, LANES)
    eq, ep = eq2.reshape(4, 54, 2, LANES), ep2.reshape(2, 18, 4, LANES)
    wq_ref, wp_ref = wq_own.reshape(54, 2, LANES), wp_own.reshape(18, 4, LANES)
    xo, dyo = x2.reshape(2, 64, 9, 2, LANES), dy2.reshape(2, 64, 9, 2, LANES)
    o_ref, dx_ref = o2.reshape(2, 64, 9, 2, LANES), d2.reshape(2, 64, 9, 2, LANES)
    wqo, wpo = wq2.reshape(8, 4, 2, 54, 2, LANES), wp2.reshape(4, 4, 2, 18, 4, LANES)
    gq_ref, gp_ref = gq2.reshape(8, 4, 2, 54, 2, LANES), gp2.reshape(4, 4, 2, 18, 4, LANES)
    pl.semaphore_wait(pltpu.get_barrier_semaphore(), 67)

    def zdev(k):
        return device((lax.rem(z + k + 8, 8) * 4 + y) * 2 + xh, d)

    def ydev(k):
        return device((z * 4 + lax.rem(y + k, 4)) * 2 + xh, d)

    def both(part, j, q_job, p_job):
        at = lax.rem(z + j, 8)
        if part == "q":
            q_job(at)
        else:
            @pl.when(lax.div(at, 4) == c)
            def _():
                p_job(lax.rem(at, 4))

    def along_z(part, j, to, there, src_q=None, src_p=None):
        both(
            part,
            j,
            lambda at: send(wqo.at[at, y, xh] if src_q is None else src_q, wqo.at[at, y, xh], ss.at[0], rz.at[0, to], there),
            lambda at: send(wpo.at[at, y, xh] if src_p is None else src_p, wpo.at[at, y, xh], ss.at[1], rz.at[1, to], there),
        )

    def z_stage(part, j):
        if j == 0:
            along_z(part, 0, 7, zdev(1), wq_ref, wp_ref)
            along_z(part, 0, 1, zdev(-1), wq_ref, wp_ref)
            both(
                part,
                0,
                lambda at: pltpu.make_async_copy(wq_ref, wqo.at[at, y, xh], rz.at[0, 0]).start(),
                lambda at: pltpu.make_async_copy(wp_ref, wpo.at[at, y, xh], rz.at[1, 0]).start(),
            )
        both(
            part,
            j,
            lambda at: wait_for(wqo.at[at, y, xh], rz.at[0, j]),
            lambda at: wait_for(wpo.at[at, y, xh], rz.at[1, j]),
        )
        if j in (7, 6):
            along_z(part, j, j - 1, zdev(1))
        if j in (1, 2):
            along_z(part, j, j + 1, zdev(-1))
        if j == 5:
            @pl.when(c == 0)
            def _():
                along_z(part, 5, 4, zdev(1))
        if j == 3:
            @pl.when(c == 1)
            def _():
                along_z(part, 3, 4, zdev(-1))

    def y_send(part, j):
        for k in (1, 3):
            both(
                part,
                j,
                lambda at: send(wqo.at[at, y, xh], wqo.at[at, y, xh], ss.at[4], ry.at[0, j, k], ydev(k)),
                lambda at: send(wpo.at[at, y, xh], wpo.at[at, y, xh], ss.at[5], ry.at[1, j, k], ydev(k)),
            )

    def across(part, j, k):
        row = lax.rem(y + 4 - k, 4)
        hq, hp = pl.ds(27 * (1 - xl), 27), pl.ds(9 * (1 - xl), 9)

        def q(at):
            ref = wqo.at[at, row, xh, hq]
            send(ref, ref, ss.at[6], rm.at[0, j, row], mirror)

        def p(at):
            ref = wpo.at[at, row, xh, hp]
            send(ref, ref, ss.at[7], rm.at[1, j, row], mirror)

        both(part, j, q, p)

    def y_wait(part, j, k):
        row = lax.rem(y + 4 - k, 4)
        both(
            part,
            j,
            lambda at: wait_for(wqo.at[at, row, xh], ry.at[0, j, k]),
            lambda at: wait_for(wpo.at[at, row, xh], ry.at[1, j, k]),
        )

    def y_pass(part, j, k):
        h = 0 if k == 1 else 1
        row = lax.rem(y + 4 - k, 4)

        def q(at):
            ref = wqo.at[at, row, xh, pl.ds(27 * h, 27)]
            send(ref, ref, ss.at[4], ry.at[0, j, 2], ydev(k))

        def p(at):
            ref = wpo.at[at, row, xh, pl.ds(9 * h, 9)]
            send(ref, ref, ss.at[5], ry.at[1, j, 2], ydev(k))

        both(part, j, q, p)

    def forward(part, j, k):
        row = lax.rem(y + 4 - k, 4)
        hq, hp = pl.ds(27 * xl, 27), pl.ds(9 * xl, 9)

        def q(at):
            ref = wqo.at[at, row, 1 - xh, hq]
            wait_for(ref, rm.at[0, j, row])
            send(ref, ref, ss.at[8], rs.at[0, j, row], side)

        def p(at):
            ref = wpo.at[at, row, 1 - xh, hp]
            wait_for(ref, rm.at[1, j, row])
            send(ref, ref, ss.at[9], rs.at[1, j, row], side)

        both(part, j, q, p)

    def lay_out(n):
        raw, line, src, dst = ((x_raw, xl2, x_ref, xo), (dy_raw, dyl2, dy_ref, dyo))[n]
        (x_fetch, dy_fetch)[n].wait()
        for i in range(6):
            line[pl.ds(i, 192, stride=6), :] = raw[:, COLS[i]]
        pltpu.make_async_copy(src.at[s], dst.at[c, s], rx.at[n]).start()

    def spread_in(n, first, last):
        src, dst = ((x_ref, xo), (dy_ref, dyo))[n]

        def one(k, carry):
            t = lax.rem(s + k, 64)
            send(src.at[t], dst.at[c, s], ss.at[2 + n], rx.at[n], device(t, d))
            return carry

        lax.fori_loop(first, last, one, 0)

    gain = gain_ref[...].reshape(1, WIDTH)
    bias = bias_ref[...].reshape(1, WIDTH)
    pbias = pbias_ref[...].reshape(1, WIDTH)

    def weights(part, j):
        at = lax.rem(z + j, 8)
        for k in range(4):
            row = lax.rem(y + 4 - k, 4)
            both(
                part,
                j,
                lambda at: wait_for(wqo.at[at, row, 1 - xh, pl.ds(27 * (1 - xl), 27)], rs.at[0, j, row]),
                lambda at: wait_for(wpo.at[at, row, 1 - xh, pl.ds(9 * (1 - xl), 9)], rs.at[1, j, row]),
            )

        def q(at):
            rows = pl.ds(pl.multiple_of(at * 96, 96), 96)
            for n in range(9):
                wh[rows, COLS[n]], wl[rows, COLS[n]] = split(wq2[pl.ds(at * 864 + n, 96, stride=9), :])

        def p(at):
            rows = pl.ds(pl.multiple_of(at * 96, 96), 96)
            for n in range(6):
                ph[rows, COLS[n]], plo[rows, COLS[n]] = split(wp2[pl.ds(at * 576 + n, 96, stride=6), :])

        both(part, j, q, p)

    def tokens(ref, g):
        base = (g // 3) * 1152 + (g % 3) * 6
        return jnp.concatenate([ref[pl.ds(base + n, 64, stride=18), :] for n in range(6)], axis=1)

    def norm(g):
        rows = slice(64 * g, 64 * (g + 1))
        v = tokens(x2, g)
        centred = v - jnp.mean(v, axis=1, keepdims=True)
        r = lax.rsqrt(jnp.mean(centred * centred, axis=1, keepdims=True) + EPSILON)
        hat = centred * r
        xhat[rows, :] = hat
        rstd[rows, :] = jnp.broadcast_to(r, (64, LANES))
        nh[rows, :], nl[rows, :] = split(hat * gain + bias)

    def cotangent(g):
        rows = slice(64 * g, 64 * (g + 1))
        v = tokens(dy2, g)
        yh[rows, :], yl[rows, :] = split(v)
        add_small(12, jnp.sum(v, axis=0, keepdims=True) * 0.5)

    def add_small(first, v):
        for n in range(6):
            at = slice(first + n, first + n + 1)
            sm[at, :] = sm[at, :] + v[:, COLS[n]]

    def query_key_value(t):
        cols = slice(HALF * t, HALF * (t + 1))
        qkv[:, cols] = mm3((nh[...], nl[...]), (wh[:, cols], wl[:, cols]), 1, 0)

    def d_attended():
        da[...] = mm3((yh[...], yl[...]), (ph[...], plo[...]), 1, 1)

    left = lax.broadcasted_iota(jnp.int32, (LANES, LANES), 1) < 64
    scale = 0.125

    def operands(rows, h):
        q = wide(split(stacked(left, qkv[rows, COLS[h]] * scale)))
        return q, split(qkv[rows, COLS[3 + h]]), split(qkv[rows, COLS[6 + h]])

    def forward_attention(i):
        rows = slice(LANES * i, LANES * (i + 1))
        first = lax.broadcasted_iota(jnp.int32, (2 * LANES, LANES), 0) % LANES < 64
        same = first == (lax.broadcasted_iota(jnp.int32, (2 * LANES, LANES), 1) < 64)
        for h in range(3):
            q, k, v = operands(rows, h)
            scores = jnp.where(same, halves(mm(q, tall(k), 1, 1)), -1e30)
            e = jnp.exp(scores - jnp.max(scores, axis=1, keepdims=True))
            probs = e / jnp.sum(e, axis=1, keepdims=True)
            pr[3 * i + h] = probs
            attended = joined_heads(left, halves(mm(wide(split(probs)), twice(v), 1, 0)))
            ah[rows, COLS[h]], al[rows, COLS[h]] = split(attended)

    def backward_attention(i):
        rows = slice(LANES * i, LANES * (i + 1))

        def over_rows(a, b):
            r = halves(mm(a, b, 0, 0))
            return r[:LANES] + r[LANES:]

        for h in range(3):
            q, k, v = operands(rows, h)
            a = wide(split(stacked(left, da[rows, COLS[h]])))
            probs = pr[3 * i + h]
            dh[rows, COLS[6 + h]], dl[rows, COLS[6 + h]] = split(over_rows(wide(split(probs)), a))
            t = halves(mm(a, tall(v), 1, 1)) * probs
            ds = wide(split(t - probs * jnp.sum(t, axis=1, keepdims=True)))
            dq = joined_heads(left, halves(mm(ds, twice(k), 1, 0))) * scale
            dh[rows, COLS[h]], dl[rows, COLS[h]] = split(dq)
            dh[rows, COLS[3 + h]], dl[rows, COLS[3 + h]] = split(over_rows(ds, q))

    def project(t):
        part = slice(HALF * t, HALF * (t + 1))
        o = mm3((ah[...], al[...]), (ph[:, part], plo[:, part]), 1, 0)
        for g in range(6):
            for n in range(3):
                at = pl.ds((g // 3) * 1152 + (g % 3) * 6 + 3 * t + n, 64, stride=18)
                own = x2[at, :] + pbias[:, COLS[3 * t + n]]
                o2[at, :] = o[64 * g : 64 * (g + 1), COLS[n]] + jnp.where(c == g // 3, own, 0.0)

    def grad_proj(t):
        part = slice(HALF * t, HALF * (t + 1))
        w = mm3((ah[...], al[...]), (yh[:, part], yl[:, part]), 0, 0)
        for n in range(3):
            gp2[pl.ds(3 * t + n, HALF, stride=6), :] = w[:, COLS[n]]

    def grad_qkv(t):
        part = slice(HALF * t, HALF * (t + 1))
        w = mm3((nh[...], nl[...]), (dh[:, part], dl[:, part]), 0, 0)
        for n in range(3):
            gq2[pl.ds(3 * t + n, WIDTH, stride=9), :] = w[:, COLS[n]]

    def grad_input(i):
        dn = mm3((dh[128 * i : 128 * (i + 1), :], dl[128 * i : 128 * (i + 1), :]), (wh[...], wl[...]), 1, 1)
        for half in range(2):
            g = 2 * i + half
            rows = slice(64 * g, 64 * (g + 1))
            n = dn[64 * half : 64 * (half + 1)]
            hat = xhat[rows, :]
            add_small(0, jnp.sum(n * hat, axis=0, keepdims=True))
            add_small(6, jnp.sum(n, axis=0, keepdims=True))
            n = n * gain
            m1 = jnp.mean(n, axis=1, keepdims=True)
            m2 = jnp.mean(n * hat, axis=1, keepdims=True)
            dx = rstd[rows, 0:1] * (n - m1 - hat * m2)
            for j in range(6):
                at = pl.ds((g // 3) * 1152 + (g % 3) * 6 + j, 64, stride=18)
                d2[at, :] = dx[:, COLS[j]] + jnp.where(c == g // 3, dy2[at, :], 0.0)

    oxh = 1 - xh
    mine_q, mine_p = pl.ds(27 * xl, 27), pl.ds(9 * xl, 9)
    yours_q, yours_p = pl.ds(27 * (1 - xl), 27), pl.ds(9 * (1 - xl), 9)

    def row(k):
        return lax.rem(y + k, 4)

    def side_send(part, j):
        for k in ROWS:
            both(
                part,
                j,
                lambda at: send(gq_ref.at[at, row(k), oxh, yours_q], r1q.at[j, k], so_sem.at[0], r1s.at[0, j, k], side),
                lambda at: send(gp_ref.at[at, row(k), oxh, yours_p], r1p.at[j, k], so_sem.at[1], r1s.at[1, j, k], side),
            )

    def mirror_send(part, j):
        for k in ROWS:
            def q(at):
                wait_for(r1q.at[j, k], r1s.at[0, j, k])
                r1q[j, k] = r1q[j, k] + gq_ref[at, row(k), oxh, mine_q]
                send(r1q.at[j, k], r2q.at[j, k], so_sem.at[5], r2s.at[0, j, k], mirror)

            def p(at):
                wait_for(r1p.at[j, k], r1s.at[1, j, k])
                r1p[j, k] = r1p[j, k] + gp_ref[at, row(k), oxh, mine_p]
                send(r1p.at[j, k], r2p.at[j, k], so_sem.at[6], r2s.at[1, j, k], mirror)

            both(part, j, q, p)

    def gather(part, j, k):
        def q(at):
            wait_for(r2q.at[j, k], r2s.at[0, j, k])
            aq[j, k, mine_q] = gq_ref[at, row(k), xh, mine_q]
            aq[j, k, yours_q] = gq_ref[at, row(k), xh, yours_q] + r2q[j, k]

        def p(at):
            wait_for(r2p.at[j, k], r2s.at[1, j, k])
            ap[j, k, mine_p] = gp_ref[at, row(k), xh, mine_p]
            ap[j, k, yours_p] = gp_ref[at, row(k), xh, yours_p] + r2p[j, k]

        both(part, j, q, p)

    def y_far(part, j):
        gather(part, j, 2)
        for n, k in ((0, 1), (1, 3)):
            both(
                part,
                j,
                lambda at: send(aq.at[j, 2, pl.ds(27 * n, 27)], hq.at[j, n], so_sem.at[10], rh.at[0, j, n], ydev(k)),
                lambda at: send(ap.at[j, 2, pl.ds(9 * n, 9)], hp.at[j, n], so_sem.at[11], rh.at[1, j, n], ydev(k)),
            )

    def y_near(part, j):
        for n, k in ((0, 1), (1, 3)):
            gather(part, j, k)

            def q(at):
                wait_for(hq.at[j, n], rh.at[0, j, n])
                piece = pl.ds(27 * n, 27)
                aq[j, k, piece] = aq[j, k, piece] + hq[j, n]
                send(aq.at[j, k], fq.at[j, n], so_sem.at[10], rf.at[0, j, n], ydev(k))

            def p(at):
                wait_for(hp.at[j, n], rh.at[1, j, n])
                piece = pl.ds(9 * n, 9)
                ap[j, k, piece] = ap[j, k, piece] + hp[j, n]
                send(ap.at[j, k], fp.at[j, n], so_sem.at[11], rf.at[1, j, n], ydev(k))

            both(part, j, q, p)

    def z_step(part, j):
        gather(part, j, 0)

        def q(at):
            wait_for(fq.at[j, 0], rf.at[0, j, 0])
            wait_for(fq.at[j, 1], rf.at[0, j, 1])
            aq[j, 0] = aq[j, 0] + (fq[j, 0] + fq[j, 1])

        def p(at):
            wait_for(fp.at[j, 0], rf.at[1, j, 0])
            wait_for(fp.at[j, 1], rf.at[1, j, 1])
            ap[j, 0] = ap[j, 0] + (fp[j, 0] + fp[j, 1])

        both(part, j, q, p)

        def come(slot):
            def q(at):
                wait_for(zq.at[slot], rzz.at[0, slot])
                aq[j, 0] = aq[j, 0] + zq[slot]

            def p(at):
                wait_for(zp.at[slot], rzz.at[1, slot])
                ap[j, 0] = ap[j, 0] + zp[slot]

            both(part, j, q, p)

        def go(slot, k):
            both(
                part,
                j,
                lambda at: send(aq.at[j, 0], zq.at[slot], so_sem.at[13], rzz.at[0, slot], zdev(k)),
                lambda at: send(ap.at[j, 0], zp.at[slot], so_sem.at[14], rzz.at[1, slot], zdev(k)),
            )

        if j == 4:
            @pl.when(c == 0)
            def _():
                go(3, 1)

            @pl.when(c == 1)
            def _():
                go(5, -1)
        elif j == 0:
            come(0)
            come(8)
        else:
            if j in (3, 5):
                @pl.when(c == (0 if j == 3 else 1))
                def _():
                    come(j)
            else:
                come(j)
            if j < 4:
                go(j - 1, 1)
            else:
                go(j + 1, -1)

    def joined(n):
        own, buf, out = ((o_ref, ob, of), (dx_ref, db, df))[n]
        wait_for(buf, rb.at[n])

        def add(i, carry):
            at = pl.ds(8 * i, 8)
            buf[at] = buf[at] + own[c, at]
            return carry

        lax.fori_loop(0, 8, add, 0)
        pltpu.make_async_copy(buf.at[s], out.at[s], ro.at[n]).start()

    def spread(n, first, last):
        buf, out = ((ob, of), (db, df))[n]

        def one(k, carry):
            t = lax.rem(s + k, 64)
            send(buf.at[t], out.at[s], so_sem.at[7 + n], ro.at[n], device(t, d))
            return carry

        lax.fori_loop(first, last, one, 0)

    def small(step):
        if step == 0:
            smx[0] = sm[...]
            send(smx.at[0], smx.at[1], so_sem.at[4], ra.at[0], mirror)
        if step == 1:
            wait_for(smx.at[1], ra.at[0])
            smy[y] = smx[0] + smx[1]
            for k in range(1, 4):
                send(smy.at[y], smy.at[y], so_sem.at[9], ra.at[1], ydev(k))
        if step == 2:
            wait_for(smy.at[pl.ds(0, 3)], ra.at[1])
            smz[z] = (smy[0] + smy[1]) + (smy[2] + smy[3])
            for k in range(1, 8):
                send(smz.at[z], smz.at[z], so_sem.at[12], ra.at[2], zdev(k))
        if step == 3:
            wait_for(smz.at[pl.ds(0, 7)], ra.at[2])
            es[d] = ((smz[0] + smz[1]) + (smz[2] + smz[3])) + ((smz[4] + smz[5]) + (smz[6] + smz[7]))
            for there in (side, mate, corner):
                send(es.at[d], es.at[d], so_sem.at[17], re.at[2], there)

    def step_in(part, t):
        if 0 <= t < 8:
            z_stage(part, ORDER[t])
            y_send(part, ORDER[t])
            across(part, ORDER[t], 0)
        if 1 <= t < 9:
            j = ORDER[t - 1]
            for k in (1, 3):
                y_wait(part, j, k)
                y_pass(part, j, k)
                across(part, j, k)
        if 2 <= t < 10:
            j = ORDER[t - 2]
            y_wait(part, j, 2)
            across(part, j, 2)
            forward(part, j, 0)
        if 3 <= t < 11:
            j = ORDER[t - 3]
            for k in (1, 3, 2):
                forward(part, j, k)
        if 6 <= t < 14:
            weights(part, ORDER[t - 6])

    def step_out(part, t):
        if 0 <= t + 1 < 8:
            side_send(part, RORDER[t + 1])
        if 0 <= t < 8:
            mirror_send(part, RORDER[t - 0])
        if 1 <= t < 9:
            y_far(part, RORDER[t - 1])
        if 2 <= t < 10:
            y_near(part, RORDER[t - 2])
        if 3 <= t < 11:
            z_step(part, RORDER[t - 3])

    for t in range(14):
        step_in("q", t)
        step_in("p", t)
        if t == 0:
            lay_out(0)
        if t == 4:
            lay_out(1)
        if t == 1:
            spread_in(0, 1, 16)
        if t == 2:
            spread_in(0, 16, 32)
        if t == 3:
            spread_in(0, 32, 48)
        if t == 4:
            spread_in(0, 48, 64)
        if t == 5:
            spread_in(1, 1, 16)
        if t == 6:
            spread_in(1, 16, 32)
        if t == 7:
            spread_in(1, 32, 48)
        if t == 8:
            spread_in(1, 48, 64)
        if t == 10:
            wait_for(xo.at[c], rx.at[0])
            send(xo.at[c], xo.at[c], ss.at[10], rc.at[0], mate)
        if t == 11:
            wait_for(dyo.at[c], rx.at[1])
            send(dyo.at[c], dyo.at[c], ss.at[11], rc.at[1], mate)
        if t == 12:
            wait_for(xo.at[1 - c], rc.at[0])
            for g in range(6):
                norm(g)
        if t == 13:
            wait_for(dyo.at[1 - c], rc.at[1])
            for g in range(6):
                cotangent(g)
        if 13 <= t < 13 + 0:
            query_key_value(t - 13)
    for t in range(0, 3):
        query_key_value(t)
    for i in range(3):
        forward_attention(i)
    project(0)
    project(1)
    send(o_ref.at[1 - c], ob, so_sem.at[2], rb.at[0], mate)
    grad_proj(0)
    grad_proj(1)
    d_attended()
    for t in range(3):
        backward_attention(t)
    for n in range(3):
        grad_qkv(n)
    for t in range(-1, 11):
        step_out("p", t)
        step_out("q", t)
        if t == 0:
            joined(0)
        if t == 1:
            spread(0, 1, 16)
        if t == 1:
            spread(0, 16, 32)
        if t == 1:
            grad_input(0)
        if t == 2:
            spread(0, 32, 48)
        if t == 2:
            spread(0, 48, 64)
        if t == 2:
            grad_input(1)
        if t == 3:
            grad_input(2)
        if t == 3:
            send(dx_ref.at[1 - c], db, so_sem.at[3], rb.at[1], mate)
        if t == 3:
            small(0)
        if t == 4:
            joined(1)
        if t == 4:
            spread(1, 1, 22)
        if t == 5:
            spread(1, 22, 43)
        if t == 5:
            small(1)
        if t == 6:
            spread(1, 43, 64)
        if t == 7:
            small(2)
        if t == 9:
            small(3)
        if t == 9:
            wait_for(ob, ro.at[0])
            for i in range(6):
                out[:, COLS[i]] = of2[pl.ds(i, 192, stride=6), :]

    eq[d] = aq[0, 0]
    for there in (side, mate, corner):
        send(eq.at[d], eq.at[d], so_sem.at[15], re.at[0], there)

    @pl.when(holds)
    def _():
        ep[xl] = ap[0, 0]
        for there in (side, mate, corner):
            send(ep.at[xl], ep.at[xl], so_sem.at[16], re.at[1], there)

    wait_for(es.at[pl.ds(0, 3)], re.at[2])
    so[...] = (es[0] + es[2]) + (es[1] + es[3])
    wait_for(eq.at[pl.ds(0, 3)], re.at[0])
    for h in range(2):
        for n in range(9):
            at = WIDTH * (n // 3) + HALF * h + LANES * (n % 3)
            rq[:, at : at + LANES] = (
                eq2[pl.ds(108 * h + n, 12, stride=9), :] + eq2[pl.ds(108 * (h + 2) + n, 12, stride=9), :]
            )

    @pl.when(holds)
    def _():
        wait_for(ep.at[0], re.at[1])

    @pl.when(jnp.logical_not(holds))
    def _():
        wait_for(ep, re.at[1])

    for n in range(6):
        rp[:, COLS[n]] = ep2[pl.ds(n, 12, stride=6), :] + ep2[pl.ds(72 + n, 12, stride=6), :]

    wait_for(db, ro.at[1])
    for i in range(6):
        dout[:, COLS[i]] = df2[pl.ds(i, 192, stride=6), :]
    wait_for(r1q, so_sem.at[0])
    wait_for(r1p.at[pl.ds(0, 4)], so_sem.at[1])
    wait_for(ob, so_sem.at[2])
    wait_for(db, so_sem.at[3])
    wait_for(smx.at[0], so_sem.at[4])
    wait_for(r2q, so_sem.at[5])
    wait_for(r2p.at[pl.ds(0, 4)], so_sem.at[6])
    wait_for(ob.at[pl.ds(0, 63)], so_sem.at[7])
    wait_for(db.at[pl.ds(0, 63)], so_sem.at[8])
    wait_for(smy.at[pl.ds(0, 3)], so_sem.at[9])
    wait_for(aq.at[:, pl.ds(0, 3)], so_sem.at[10])
    wait_for(ap.at[pl.ds(0, 4), pl.ds(0, 3)], so_sem.at[11])
    wait_for(smz.at[pl.ds(0, 7)], so_sem.at[12])
    wait_for(zq.at[pl.ds(0, 7)], so_sem.at[13])
    wait_for(eq.at[pl.ds(0, 3)], so_sem.at[15])
    wait_for(es.at[pl.ds(0, 3)], so_sem.at[17])

    @pl.when(holds)
    def _():
        wait_for(zp.at[pl.ds(0, 3)], so_sem.at[14])
        wait_for(zp.at[pl.ds(0, 3)], so_sem.at[16])

    @pl.when(jnp.logical_not(holds))
    def _():
        wait_for(zp.at[pl.ds(0, 4)], so_sem.at[14])
    wait_for(wqo.at[pl.ds(0, 7), 0, 0], ss.at[0])
    z_sends = (0, 7, 6, 0, 1, 2)
    for j in z_sends:
        @pl.when(lax.div(lax.rem(z + j, 8), 4) == c)
        def _():
            wait_for(wp_ref, ss.at[1])
    for j, core in ((5, 0), (3, 1)):
        @pl.when(jnp.logical_and(c == core, lax.div(lax.rem(z + j, 8), 4) == c))
        def _():
            wait_for(wp_ref, ss.at[1])
    wait_for(xo.at[0, pl.ds(0, 63)], ss.at[2])
    wait_for(xo.at[0, pl.ds(0, 63)], ss.at[3])
    wait_for(wqo.at[:, pl.ds(0, 3), 0], ss.at[4])
    wait_for(wpo.at[:, pl.ds(0, 3), 0], ss.at[5])
    for sem in (6, 8):
        wait_for(wqo.at[:, :, 0, pl.ds(0, 27)], ss.at[sem])
    for sem in (7, 9):
        wait_for(wpo.at[:, :, 0, pl.ds(0, 9)], ss.at[sem])
    wait_for(xo.at[0], ss.at[10])
    wait_for(xo.at[0], ss.at[11])


def layer(x, dy, wq, wp, gain, bias, pbias):
    dma = pltpu.SemaphoreType.DMA
    vmem = pl.BlockSpec(memory_space=pltpu.VMEM)
    act, sml = (64, 9, 2, LANES), (24, LANES)
    q, p = (54, 2, LANES), (18, 4, LANES)
    q2, p2 = (27, 2, LANES), (9, 4, LANES)
    n = HALF

    def buf(*shape):
        return pltpu.VMEM(shape, F32)

    def low(*shape):
        return pltpu.VMEM(shape, BF16)

    return pl.pallas_call(
        layer_kernel,
        out_shape=(
            jax.ShapeDtypeStruct((192, WIDTH), F32),
            jax.ShapeDtypeStruct((192, WIDTH), F32),
            jax.ShapeDtypeStruct((12, 3 * WIDTH), F32),
            jax.ShapeDtypeStruct((12, WIDTH), F32),
            jax.ShapeDtypeStruct(sml, F32),
        ),
        in_specs=[pl.BlockSpec(memory_space=pl.ANY)] * 2 + [vmem] * 5,
        out_specs=(vmem,) * 5,
        scratch_shapes=[
            buf(192, WIDTH), buf(192, WIDTH), dma((2,)),
            buf(1152, LANES), buf(1152, LANES), buf(1152, LANES), buf(1152, LANES), buf(432, LANES), buf(144, LANES),
            buf(108, LANES), buf(72, LANES),
            buf(2304, LANES), buf(2304, LANES), buf(6912, LANES), buf(2304, LANES),
            buf(n, WIDTH), buf(n, LANES), low(n, WIDTH), low(n, WIDTH), low(n, WIDTH), low(n, WIDTH),
            low(WIDTH, 3 * HALF), low(WIDTH, 3 * HALF), low(HALF, WIDTH), low(HALF, WIDTH),
            buf(n, 3 * HALF), buf(n, HALF), low(n, HALF), low(n, HALF), low(n, 3 * HALF), low(n, 3 * HALF),
            buf(2304, LANES), buf(2304, LANES), buf(6912, LANES), buf(2304, LANES), buf(*sml), buf(9, 2 * LANES, LANES),
            buf(*act), buf(*act),
            buf(8, 4, *q2), buf(8, 4, *p2), buf(8, 4, *q2), buf(8, 4, *p2),
            buf(8, 4, *q), buf(8, 4, *p), buf(8, 2, *q2), buf(8, 2, *p2), buf(8, 2, *q), buf(8, 2, *p),
            buf(9, *q), buf(9, *p), buf(4, *sml),
            buf(2, *sml), buf(4, *sml), buf(8, *sml),
            dma((12,)), dma((2,)), dma((2, 8)), dma((2, 8, 4)), dma((2, 8, 4)), dma((2, 8, 4)), dma((2,)),
            dma((18,)), dma((2,)), dma((2, 8, 4)), dma((2, 8, 4)), dma((2, 8, 2)), dma((2, 8, 2)), dma((2, 9)),
            dma((2,)), dma((3,)), dma((3,)),
        ],
        compiler_params=pltpu.CompilerParams(
            collective_id=0, has_side_effects=True, vmem_limit_bytes=56 * 1024 * 1024
        ),
    )(x, dy, wq, wp, gain, bias, pbias)


def on_device(
    frames, out_cotangent, layer_norm_gain, layer_norm_bias, qkv_weight, proj_weight, proj_bias
):
    out, dout, rq, rp, so = layer(
        frames.reshape(192, WIDTH),
        out_cotangent.reshape(192, WIDTH),
        qkv_weight,
        proj_weight,
        layer_norm_gain,
        layer_norm_bias,
        proj_bias,
    )
    sums = so[:18].reshape(3, WIDTH)
    return (
        out.reshape(frames.shape),
        dout.reshape(frames.shape),
        sums[0],
        sums[1],
        rq,
        rp,
        sums[2],
    )


def solution(mesh):
    return jax.shard_map(
        on_device,
        mesh=mesh,
        in_specs=(
            P("dp", "seq", None, None),
            P("dp", "seq", None, None),
            P(),
            P(),
            P("seq", None),
            P("seq", None),
            P(),
        ),
        out_specs=(
            P("dp", "seq", None, None),
            P("dp", "seq", None, None),
            P(),
            P(),
            P("seq", None),
            P("seq", None),
            P(),
        ),
        check_vma=False,
    )
```
